32 devices in a mesh: parts: 2 (over y), wide: 8 (over z, x), narrow: 2 (over core).
Axes of the slice: x: 2, y: 2, z: 4, core: 2. Of those that a mesh axis runs over, the one named last changes fastest.
Arguments:
- right_side: float32 [32768, 512], P(('parts', 'wide', 'narrow')), parts along dimension 0, may hold values from -6 to 6
- leaf_inverse: float32 [32768, 1024], P(('parts', 'wide', 'narrow')), parts along dimension 0, may hold values from -0.1875 to 0.1875
- row_bases: float32 [3, 32768, 128], P(None, ('parts', 'wide', 'narrow')), parts along dimension 1, may hold values from -0.5 to 0.5
- dual_bases: float32 [3, 32768, 128], P(None, ('parts', 'wide', 'narrow')), parts along dimension 1, may hold values from -0.0625 to 0.0625
- woodbury_cores: float32 [3584, 256], P('parts'), parts along dimension 0, may hold values from -0.375 to 0.375
Outputs:
- solution: float32 [32768, 512], P(('parts', 'wide', 'narrow')), parts along dimension 0
The draws below stay inside these ranges and needn't reach their ends.
There are 2 independent parts, one for each index of `parts`. The reference program is written for one: setup_inputs(seed, part) draws one part's arguments, and reference() takes and returns one part's arrays. A program takes and returns all parts, laid end to end along the dimension named above; each array names one. Nothing has to cross between parts.
All inputs are finite; a program needn't handle non-finite values.
Results may differ from the reference program's by a relative error of at most 0.00011.
Values sent between devices are 32-bit elements; how exact they have to be, the bound alone decides.
No kernel may reach another device: no remote copies, remote signals or barrier semaphores. Data moves between devices by JAX's collectives and lax.ppermute only.
A program may use at most 128 MiB of HBM per device.

```python
import jax
import jax.numpy as jnp
from jax import lax

ROWS_DEV = 1024
NRHS = 512
RANK = 128
LEVELS = 3
NROWS = 16384
CHILDREN = 14
N_WIDE = 8
N_NARROW = 2


def steps_of(rng, extent, cuts, low, high):
    def one(position, parts):
        steps = jax.random.uniform(jax.random.fold_in(jax.random.fold_in(rng, 6), position), (parts,), jnp.float32, low / len(cuts), high / len(cuts))
        return jnp.repeat(jnp.exp(steps), extent[position] // parts).reshape((-1,) + (1,) * (len(extent) - position - 1))

    gain = one(*cuts[0])
    for cut in cuts[1:]:
        gain = gain * one(*cut)
    return gain


def centred(own_key, dims, width, bound, cuts=(), dtype=jnp.bfloat16):
    array = width * jax.random.normal(own_key, dims, jnp.float32)
    if cuts:
        array = array * steps_of(own_key, dims, cuts, -0.22, 0.18)
    return jnp.clip(array, -bound, bound).astype(dtype)


def setup_inputs(seed: int = 0, part: int = 0) -> dict:
    streams_of = jax.random.split(jax.random.key(seed), 6)
    part_keys = jax.random.split(jax.random.fold_in(streams_of[5], part), 6)
    return {
        "right_side": centred(part_keys[0], (NROWS, NRHS), 1.0, 6.0, ((0, 16),), jnp.float32),
        "leaf_inverse": centred(part_keys[1], (NROWS, ROWS_DEV), ROWS_DEV ** -0.5, 0.1875, ((0, 16),), jnp.float32),
        "row_bases": centred(part_keys[2], (LEVELS, NROWS, RANK), RANK ** -0.5, 0.5, ((1, 16),), jnp.float32),
        "dual_bases": centred(part_keys[3], (LEVELS, NROWS, RANK), (NROWS // 2) ** -0.5, 0.0625, ((1, 16),), jnp.float32),
        "woodbury_cores": centred(part_keys[4], (CHILDREN * RANK, 2 * RANK), (2 * RANK) ** -0.5, 0.375, (), jnp.float32),
    }


def reference(right_side, leaf_inverse, row_bases, dual_bases, woodbury_cores):
    highest = lax.Precision.HIGHEST
    groups = N_WIDE * N_NARROW
    blocks = right_side.reshape(groups, ROWS_DEV, NRHS)
    leaves = leaf_inverse.reshape(groups, ROWS_DEV, ROWS_DEV)
    field = jnp.einsum("gij,gjn->gin", leaves, blocks, precision=highest)
    field = field.reshape(NROWS, NRHS)
    for level in range(LEVELS, 0, -1):
        count = 2 ** level
        length = NROWS // count
        pieces = field.reshape(count, length, NRHS)
        duals = dual_bases[level - 1].reshape(count, length, RANK)
        lefts = row_bases[level - 1].reshape(count, length, RANK)
        projection = jnp.einsum("csk,csn->ckn", duals, pieces, precision=highest)
        paired = projection.reshape(count // 2, 2 * RANK, NRHS)
        stacked = jnp.repeat(paired, 2, axis=0)
        cores = woodbury_cores[(count - 2) * RANK:(2 * count - 2) * RANK].reshape(count, RANK, 2 * RANK)
        coefficient = jnp.einsum("ckj,cjn->ckn", cores, stacked, precision=highest)
        pieces = pieces - jnp.einsum("csk,ckn->csn", lefts, coefficient, precision=highest)
        field = pieces.reshape(NROWS, NRHS)
    return field
```

```python
import jax
import jax.numpy as jnp
from jax import lax
from jax.sharding import PartitionSpec as P

PRECISION = lax.Precision.HIGH


def mul(a, b):
    return jnp.dot(a, b, precision=PRECISION, preferred_element_type=jnp.float32)


def mul_t(a, b):
    return lax.dot_general(
        a, b, (((0,), (0,)), ((), ())), precision=PRECISION, preferred_element_type=jnp.float32
    )


def swap_wide(block, bit):
    count = lax.axis_size("wide")
    return lax.ppermute(block, "wide", [(w, w ^ (1 << bit)) for w in range(count)])


def swap_narrow(block):
    return lax.ppermute(block, "narrow", [(0, 1), (1, 0)])


def swap_crossed(block, first, second):
    wides, cores = lax.axis_size("wide"), lax.axis_size("narrow")
    route = []
    for w in range(wides):
        for n in range(cores):
            bit = first if n == 0 else second
            route.append((w * cores + n, (w ^ (1 << bit)) * cores + n))
    return lax.ppermute(block, ("wide", "narrow"), route)


def ordered(slot, own, other, axis=0):
    return jnp.where(
        slot == 0,
        jnp.concatenate([own, other], axis),
        jnp.concatenate([other, own], axis),
    )


def shards(right_side, leaf_inverse, row_bases, dual_bases, woodbury_cores):
    rank = row_bases.shape[2]
    rows = row_bases.shape[1]
    cols = right_side.shape[1]
    half = cols // 2
    depth = lax.axis_size("wide").bit_length() - 1
    rest = depth - 3
    bit3, bit2, bit1 = rest, rest + 1, rest + 2
    child = jnp.right_shift(lax.axis_index("wide"), rest)
    pair, side = jnp.right_shift(child, 1), jnp.right_shift(child, 2)
    slot3, slot2, slot1 = jnp.bitwise_and(child, 1), jnp.bitwise_and(pair, 1), side
    core = lax.axis_index("narrow")

    m13, m23 = mul_t(dual_bases[0], row_bases[2]), mul_t(dual_bases[1], row_bases[2])
    m12 = mul_t(dual_bases[0], row_bases[1])
    m = jnp.concatenate([m23, m13, m12], 0)
    for bit in range(rest):
        m = m + swap_wide(m, bit)
    m_other = swap_wide(m, bit3)
    m12_pair = m[2 * rank:] + m_other[2 * rank:]
    m12_other = swap_wide(m12_pair, bit2)
    cores3 = lax.dynamic_slice_in_dim(woodbury_cores, (3 + pair) * 2 * rank, 2 * rank, 0)
    cores2 = lax.dynamic_slice_in_dim(woodbury_cores, (1 + side) * 2 * rank, 2 * rank, 0)
    cores1 = woodbury_cores[: 2 * rank]
    bf = mul(
        ordered(slot3, m[: 2 * rank], m_other[: 2 * rank], 1),
        lax.dynamic_slice_in_dim(cores3, slot3 * rank, rank, 1),
    )
    e = mul(
        ordered(slot2, m12_pair, m12_other, 1),
        lax.dynamic_slice_in_dim(cores2, slot2 * rank, rank, 1),
    )
    bfe = jnp.concatenate([bf, e], 0)
    bfe = bfe + swap_narrow(bfe)

    duals = jnp.concatenate([dual_bases[0], dual_bases[1], dual_bases[2]], 1)
    g = mul_t(duals, leaf_inverse)
    keep = lax.dynamic_slice_in_dim(right_side, core * half, half, 1)
    send = lax.dynamic_slice_in_dim(right_side, (1 - core) * half, half, 1)
    q = mul(g, keep) + swap_narrow(mul(g, send))
    for bit in range(rest):
        q = q + swap_wide(q, bit)
    q1, q2, q3 = q[:rank], q[rank: 2 * rank], q[2 * rank:]
    v = q2 - mul(bfe[:rank], q3)
    w = q1 - mul(bfe[rank: 2 * rank], q3) - mul(bfe[2 * rank:], v)

    w = w + swap_crossed(w, bit2, bit3)
    w = w + swap_crossed(w, bit3, bit2)
    w_other = swap_wide(w, bit1)
    k1 = mul(
        lax.dynamic_slice_in_dim(cores1, slot1 * rank, rank, 0), ordered(slot1, w, w_other)
    )
    v = v + swap_wide(v, bit3)
    v_other = swap_wide(v, bit2)
    k2 = mul(
        lax.dynamic_slice_in_dim(cores2, slot2 * rank, rank, 0), ordered(slot2, v, v_other)
    )
    q_other = swap_wide(q3, bit3)
    k3 = mul(
        lax.dynamic_slice_in_dim(cores3, slot3 * rank, rank, 0), ordered(slot3, q3, q_other)
    )

    k23 = jnp.concatenate([k2, k3], 0)
    k23_other = swap_narrow(k23)
    k1_other = swap_narrow(k1)
    field = mul(leaf_inverse, right_side)
    lefts = jnp.concatenate([row_bases[1], row_bases[2]], 1)
    field = field - mul(lefts, ordered(core, k23, k23_other, 1))
    return field - mul(row_bases[0], ordered(core, k1, k1_other, 1))


def solution(mesh):
    return jax.shard_map(
        shards,
        mesh=mesh,
        in_specs=(
            P(("parts", "wide", "narrow"), None),
            P(("parts", "wide", "narrow"), None),
            P(None, ("parts", "wide", "narrow"), None),
            P(None, ("parts", "wide", "narrow"), None),
            P("parts", None),
        ),
        out_specs=P(("parts", "wide", "narrow"), None),
        check_vma=False,
    )
```

```python
import functools

import jax
import jax.numpy as jnp
from jax import lax
from jax.experimental import pallas as pl
from jax.experimental.pallas import tpu as pltpu
from jax.sharding import PartitionSpec as P

F32, BF16 = jnp.float32, jnp.bfloat16
VMEM = pl.BlockSpec(memory_space=pltpu.VMEM)


def dot(a, b):
    return jnp.dot(a, b, precision=lax.Precision.HIGH, preferred_element_type=F32)


def dot_t(a, b):
    return lax.dot_general(
        a, b, (((0,), (0,)), ((), ())), precision=lax.Precision.HIGH, preferred_element_type=F32
    )


def halves(x):
    high = x.astype(BF16)
    return high, (x - high.astype(F32)).astype(BF16)


def dot3(a, b):
    def one(x, y):
        return jnp.dot(x, y, preferred_element_type=F32)

    return one(a[0], b[0]) + one(a[0], b[1]) + one(a[1], b[0])


def shape(*dims, dtype=F32):
    return jax.ShapeDtypeStruct(dims, dtype)


def call(body, outs, args, flops, scratch=(), aliases=None, out_specs=None):
    bytes_accessed = sum(a.size * a.dtype.itemsize for a in args)
    return pl.pallas_call(
        body,
        in_specs=[VMEM] * len(args),
        out_specs=jax.tree.map(lambda _: VMEM, outs) if out_specs is None else out_specs,
        out_shape=outs,
        scratch_shapes=list(scratch),
        input_output_aliases=aliases or {},
        compiler_params=pltpu.CompilerParams(vmem_limit_bytes=24 * 2**20),
        cost_estimate=pl.CostEstimate(
            flops=flops, bytes_accessed=bytes_accessed // 4, transcendentals=0
        ),
    )(*args)


def place(rest):
    child = lax.shift_right_logical(lax.axis_index("wide"), rest)
    return child, lax.axis_index("narrow")


def block(index, size):
    return pl.ds(pl.multiple_of(index * size, size), size)


def base_products(dual_ref, row_ref, pairs_ref, last_ref):
    rank = row_ref.shape[2]
    pairs_ref[:rank] = dot_t(dual_ref[1], row_ref[2])
    pairs_ref[rank:] = dot_t(dual_ref[0], row_ref[2])
    last_ref[...] = dot_t(dual_ref[0], row_ref[1])


def leaf_rows(start, leaf_ref, right_ref, field_ref):
    rows = field_ref.shape[0]
    step = min(256, rows)
    right = halves(right_ref[...])
    for i in range(0, rows, step):
        field_ref[i:i + step] = dot3(halves(leaf_ref[start + i:start + i + step]), right)


def projections(rest, dual_ref, first_ref, last_ref, keep_ref, send_ref, high_ref, low_ref):
    levels, rows, rank = dual_ref.shape
    for l in range(levels):
        high, low = halves(dual_ref[l].T)
        high_ref[l * rank:(l + 1) * rank] = high
        low_ref[l * rank:(l + 1) * rank] = low
    _, core = place(rest)
    half = keep_ref.shape[1]
    cut = first_ref.shape[0]
    for out, index in ((keep_ref, core), (send_ref, 1 - core)):
        cols = block(index, half)
        top, bottom = halves(first_ref[:, cols]), halves(last_ref[:, cols])
        out[...] = dot3((high_ref[:, :cut], low_ref[:, :cut]), top) + dot3(
            (high_ref[:, cut:], low_ref[:, cut:]), bottom
        )


def corrections(rest, pairs_ref, pairs_x_ref, last_ref, last_x_ref, last_z_ref, cores_ref, out_ref):
    rank = last_ref.shape[0]
    child, _ = place(rest)
    pair = lax.shift_right_logical(child, 1)
    slot3, slot2 = child & 1, pair & 1
    own = cores_ref[block(6 + child, rank), block(slot3, rank)]
    other = cores_ref[block(6 + (child ^ 1), rank), block(slot3, rank)]
    out_ref[:2 * rank] = dot(pairs_ref[...], own) + dot(pairs_x_ref[...], other)
    own = cores_ref[block(2 + pair, rank), block(slot2, rank)]
    other = cores_ref[block(2 + (pair ^ 1), rank), block(slot2, rank)]
    out_ref[2 * rank:] = dot(last_ref[...] + last_x_ref[...], own) + dot(last_z_ref[...], other)


def corrected(keep_ref, recv_ref, fix_ref, fix_other_ref, w_ref, v_ref):
    rank = w_ref.shape[0]
    q = keep_ref[...] + recv_ref[...]
    fix = fix_ref[...] + fix_other_ref[...]
    q1, q2, q3 = q[:rank], q[rank:2 * rank], q[2 * rank:]
    both = dot(fix[:2 * rank], q3)
    v = q2 - both[:rank]
    w_ref[...] = q1 - both[rank:] - dot(fix[2 * rank:], v)
    v_ref[:rank] = v
    v_ref[rank:] = q3


def lower_coefficients(rest, v_ref, vq_ref, vz_ref, vqx_ref, cores_ref, out_ref):
    rank = vz_ref.shape[0]
    child, _ = place(rest)
    pair = lax.shift_right_logical(child, 1)
    slot3, slot2 = child & 1, pair & 1
    rows2, rows3 = block(2 + pair, rank), block(6 + child, rank)
    out_ref[:rank] = dot(cores_ref[rows2, block(slot2, rank)], v_ref[...]) + dot(
        cores_ref[rows2, block(1 - slot2, rank)], vz_ref[...]
    )
    out_ref[rank:] = dot(cores_ref[rows3, block(slot3, rank)], vq_ref[rank:]) + dot(
        cores_ref[rows3, block(1 - slot3, rank)], vqx_ref[rank:]
    )


def lower_update(rest, first_ref, last_ref, row_ref, k_ref, k_other_ref, out_ref):
    rank = row_ref.shape[2]
    cut = first_ref.shape[0]
    half = k_ref.shape[1]
    _, core = place(rest)
    lefts = jnp.concatenate([row_ref[1], row_ref[2]], 1)
    for ref, index in ((k_ref, core), (k_other_ref, 1 - core)):
        cols = block(index, half)
        term = dot(lefts, ref[...])
        out_ref[:cut, cols] = first_ref[:, cols] - term[:cut]
        out_ref[cut:, cols] = last_ref[:, cols] - term[cut:]


def top_coefficient(rest, w, w_far, cores_ref):
    rank = w.shape[0]
    child, _ = place(rest)
    slot1 = lax.shift_right_logical(child, 2)
    rows1 = block(slot1, rank)
    return dot(cores_ref[rows1, block(slot1, rank)], w) + dot(
        cores_ref[rows1, block(1 - slot1, rank)], w_far
    )


def top_own(rest, field_ref, row_ref, w_ref, w_far_ref, cores_ref, out_ref):
    _, core = place(rest)
    cols = block(core, w_ref.shape[1])
    k = top_coefficient(rest, w_ref[...], w_far_ref[...], cores_ref)
    out_ref[...] = field_ref[:, cols] - dot(row_ref[0], k)


def top_other(rest, chunks, field_ref, own_ref, row_ref, w_ref, w_far_ref, cores_ref, out_ref, other_ref, sems):
    _, core = place(rest)
    rows, half = own_ref.shape
    mine, theirs = block(core, half), block(1 - core, half)
    copies = [pltpu.make_async_copy(own_ref, out_ref.at[:, mine], sems.at[chunks])]
    copies[0].start()
    k = top_coefficient(rest, w_ref[...], w_far_ref[...], cores_ref)
    step = rows // chunks
    for i in range(chunks):
        part = slice(i * step, (i + 1) * step)
        other_ref[part] = field_ref[part, theirs] - dot(row_ref[0, part], k)
        copy = pltpu.make_async_copy(other_ref.at[part], out_ref.at[part, theirs], sems.at[i])
        copy.start()
        copies.append(copy)
    for copy in copies:
        copy.wait()


def swap_wide(x, bit):
    count = lax.axis_size("wide")
    return lax.ppermute(x, "wide", [(w, w ^ (1 << bit)) for w in range(count)])


def swap_narrow(x):
    return lax.ppermute(x, "narrow", [(0, 1), (1, 0)])


def swap_crossed(x, first, second):
    wides, cores = lax.axis_size("wide"), lax.axis_size("narrow")
    route = []
    for w in range(wides):
        for n in range(cores):
            bit = first if n == 0 else second
            route.append((w * cores + n, (w ^ (1 << bit)) * cores + n))
    return lax.ppermute(x, ("wide", "narrow"), route)


def shards(right_side, leaf_inverse, row_bases, dual_bases, woodbury_cores):
    levels, rows, rank = row_bases.shape
    cols = right_side.shape[1]
    half = cols // 2
    rest = lax.axis_size("wide").bit_length() - 1 - levels
    bit3, bit2, bit1 = rest, rest + 1, rest + 2
    cut = rows * 3 // 4

    pairs, last = call(
        base_products, (shape(2 * rank, rank), shape(rank, rank)), (dual_bases, row_bases),
        6 * rows * rank * rank,
    )
    for bit in range(rest):
        pairs, last = pairs + swap_wide(pairs, bit), last + swap_wide(last, bit)
    last_x, pairs_x = swap_wide(last, bit3), swap_wide(pairs, bit3)

    first_rows = call(
        functools.partial(leaf_rows, 0), shape(cut, cols), (leaf_inverse, right_side),
        6 * cut * rows * cols,
    )
    last_z = swap_wide(last + last_x, bit2)
    last_rows = call(
        functools.partial(leaf_rows, cut), shape(rows - cut, cols), (leaf_inverse, right_side),
        6 * (rows - cut) * rows * cols,
    )
    keep, send = call(
        functools.partial(projections, rest), (shape(levels * rank, half),) * 2,
        (dual_bases, first_rows, last_rows), 6 * levels * rank * rows * cols,
        scratch=[pltpu.VMEM((levels * rank, rows), BF16)] * 2,
    )
    recv = swap_narrow(send)
    fix = call(
        functools.partial(corrections, rest), shape(levels * rank, rank),
        (pairs, pairs_x, last, last_x, last_z, woodbury_cores), 36 * rank**3,
    )
    fix_other = swap_narrow(fix)
    if rest:
        keep = keep + recv
        for bit in range(rest):
            keep = keep + swap_wide(keep, bit)
        recv = jnp.zeros_like(keep)
    w, vq = call(
        corrected, (shape(rank, half), shape(2 * rank, half)), (keep, recv, fix, fix_other),
        18 * rank * rank * half,
    )

    w = w + swap_crossed(w, bit2, bit3)
    vq_x = swap_wide(vq, bit3)
    w = w + swap_crossed(w, bit3, bit2)
    w_far = swap_wide(w, bit1)
    v = vq[:rank] + vq_x[:rank]
    v_z = swap_wide(v, bit2)
    k = call(
        functools.partial(lower_coefficients, rest), shape(2 * rank, half),
        (v, vq, v_z, vq_x, woodbury_cores), 24 * rank * rank * half,
    )
    k_other = swap_narrow(k)
    w_other = swap_narrow(w)
    field = call(
        functools.partial(lower_update, rest), shape(rows, cols),
        (first_rows, last_rows, row_bases, k, k_other), 12 * rows * rank * cols,
    )
    w_far_other = swap_narrow(w_far)
    own = call(
        functools.partial(top_own, rest), shape(rows, half),
        (field, row_bases, w, w_far, woodbury_cores), 6 * rows * rank * half,
    )
    chunks = 2
    return call(
        functools.partial(top_other, rest, chunks), shape(rows, cols),
        (field, own, row_bases, w_other, w_far_other, woodbury_cores), 6 * rows * rank * half,
        scratch=[pltpu.VMEM((rows, half), F32), pltpu.SemaphoreType.DMA((chunks + 1,))],
        out_specs=pl.BlockSpec(memory_space=pltpu.HBM),
    )


def solution(mesh):
    return jax.shard_map(
        shards,
        mesh=mesh,
        in_specs=(
            P(("parts", "wide", "narrow"), None),
            P(("parts", "wide", "narrow"), None),
            P(None, ("parts", "wide", "narrow"), None),
            P(None, ("parts", "wide", "narrow"), None),
            P("parts", None),
        ),
        out_specs=P(("parts", "wide", "narrow"), None),
        check_vma=False,
    )
```

```python
import functools

import jax
import jax.numpy as jnp
from jax import lax
from jax.experimental import pallas as pl
from jax.experimental.pallas import tpu as pltpu
from jax.sharding import PartitionSpec as P

F32, BF16 = jnp.float32, jnp.bfloat16
VMEM = pl.BlockSpec(memory_space=pltpu.VMEM)


def dot(a, b):
    return jnp.dot(a, b, precision=lax.Precision.HIGH, preferred_element_type=F32)


def dot_t(a, b):
    return lax.dot_general(
        a, b, (((0,), (0,)), ((), ())), precision=lax.Precision.HIGH, preferred_element_type=F32
    )


def halves(x):
    high = x.astype(BF16)
    return high, (x - high.astype(F32)).astype(BF16)


def dot3(a, b):
    def one(x, y):
        return jnp.dot(x, y, preferred_element_type=F32)

    return one(a[0], b[0]) + one(a[0], b[1]) + one(a[1], b[0])


def shape(*dims, dtype=F32):
    return jax.ShapeDtypeStruct(dims, dtype)


def call(body, outs, args, flops, in_specs=None, scratch=(), aliases=None, out_specs=None):
    bytes_accessed = sum(a.size * a.dtype.itemsize for a in args)
    return pl.pallas_call(
        body,
        in_specs=in_specs or [VMEM] * len(args),
        out_specs=jax.tree.map(lambda _: VMEM, outs) if out_specs is None else out_specs,
        out_shape=outs,
        scratch_shapes=list(scratch),
        input_output_aliases=aliases or {},
        compiler_params=pltpu.CompilerParams(vmem_limit_bytes=24 * 2**20),
        cost_estimate=pl.CostEstimate(
            flops=flops, bytes_accessed=0, transcendentals=0
        ),
    )(*args)


def place(rest):
    child = lax.shift_right_logical(lax.axis_index("wide"), rest)
    return child, lax.axis_index("narrow")


def block(index, size):
    return pl.ds(pl.multiple_of(index * size, size), size)


def base_products(dual_hbm, row_hbm, pairs_ref, last_ref, dual_ref, row_ref, sems):
    rank = row_hbm.shape[2]
    sources = (dual_hbm.at[0], row_hbm.at[1], row_hbm.at[2], dual_hbm.at[1])
    targets = (dual_ref.at[0], row_ref.at[0], row_ref.at[1], dual_ref.at[1])
    copies = [
        pltpu.make_async_copy(source, target, sems.at[i])
        for i, (source, target) in enumerate(zip(sources, targets))
    ]
    for copy in copies:
        copy.start()
    copies[0].wait()
    copies[1].wait()
    last_ref[...] = dot_t(dual_ref[0], row_ref[0])
    copies[2].wait()
    pairs_ref[rank:] = dot_t(dual_ref[0], row_ref[1])
    copies[3].wait()
    pairs_ref[:rank] = dot_t(dual_ref[1], row_ref[1])


def leaf_rows(start, leaf_ref, right_ref, field_ref):
    rows = field_ref.shape[0]
    step = min(256, rows)
    right = halves(right_ref[...])
    for i in range(0, rows, step):
        field_ref[i:i + step] = dot3(halves(leaf_ref[start + i:start + i + step]), right)


def projections(rest, dual_ref, first_ref, last_ref, keep_ref, send_ref, high_ref, low_ref):
    levels, rows, rank = dual_ref.shape
    for l in range(levels):
        high, low = halves(dual_ref[l].T)
        high_ref[l * rank:(l + 1) * rank] = high
        low_ref[l * rank:(l + 1) * rank] = low
    _, core = place(rest)
    half = keep_ref.shape[1]
    cut = first_ref.shape[0]
    for out, index in ((keep_ref, core), (send_ref, 1 - core)):
        cols = block(index, half)
        top, bottom = halves(first_ref[:, cols]), halves(last_ref[:, cols])
        out[...] = dot3((high_ref[:, :cut], low_ref[:, :cut]), top) + dot3(
            (high_ref[:, cut:], low_ref[:, cut:]), bottom
        )


def corrections(rest, pairs_ref, pairs_x_ref, last_ref, last_x_ref, last_z_ref, cores_ref, out_ref):
    rank = last_ref.shape[0]
    child, _ = place(rest)
    pair = lax.shift_right_logical(child, 1)
    slot3, slot2 = child & 1, pair & 1
    own = cores_ref[block(6 + child, rank), block(slot3, rank)]
    other = cores_ref[block(6 + (child ^ 1), rank), block(slot3, rank)]
    out_ref[:2 * rank] = dot(pairs_ref[...], own) + dot(pairs_x_ref[...], other)
    own = cores_ref[block(2 + pair, rank), block(slot2, rank)]
    other = cores_ref[block(2 + (pair ^ 1), rank), block(slot2, rank)]
    out_ref[2 * rank:] = dot(last_ref[...] + last_x_ref[...], own) + dot(last_z_ref[...], other)


def corrected(keep_ref, recv_ref, fix_ref, fix_other_ref, *out_refs):
    *w_refs, v_ref, q_ref = out_refs
    rank = v_ref.shape[0]
    q = keep_ref[...] + recv_ref[...]
    fix = fix_ref[...] + fix_other_ref[...]
    q1, q2, q3 = q[:rank], q[rank:2 * rank], q[2 * rank:]
    both = dot(fix[:2 * rank], q3)
    v = q2 - both[:rank]
    w = q1 - both[rank:] - dot(fix[2 * rank:], v)
    width = w.shape[1] // len(w_refs)
    for i, w_ref in enumerate(w_refs):
        w_ref[...] = w[:, i * width:(i + 1) * width]
    v_ref[...] = v
    q_ref[...] = q3


def lower_coefficients(rest, v_ref, vz_ref, q_ref, qx_ref, cores_ref, out_ref):
    rank = vz_ref.shape[0]
    child, _ = place(rest)
    pair = lax.shift_right_logical(child, 1)
    slot3, slot2 = child & 1, pair & 1
    rows2, rows3 = block(2 + pair, rank), block(6 + child, rank)
    out_ref[:rank] = dot(cores_ref[rows2, block(slot2, rank)], v_ref[...]) + dot(
        cores_ref[rows2, block(1 - slot2, rank)], vz_ref[...]
    )
    out_ref[rank:] = dot(cores_ref[rows3, block(slot3, rank)], q_ref[...]) + dot(
        cores_ref[rows3, block(1 - slot3, rank)], qx_ref[...]
    )


def solved(rest, chunk, index, first_ref, last_ref, row_ref, k_ref, w_ref, far_ref, cores_ref):
    levels, _, rank = row_ref.shape
    width = w_ref.shape[1]
    child, _ = place(rest)
    slot1 = lax.shift_right_logical(child, 2)
    rows1 = block(slot1, rank)
    top = dot(cores_ref[rows1, block(slot1, rank)], w_ref[...]) + dot(
        cores_ref[rows1, block(1 - slot1, rank)], far_ref[...]
    )
    part = slice(chunk * width, (chunk + 1) * width)
    coefficients = jnp.concatenate([top, k_ref[:, part]], 0)
    cols = block(index * (k_ref.shape[1] // width) + chunk, width)
    cut = first_ref.shape[0]

    def rows(start, stop):
        lefts = jnp.concatenate([row_ref[l, start:stop] for l in range(levels)], 1)
        term = dot(lefts, coefficients)
        if start < cut:
            return first_ref[start:stop, cols] - term
        return last_ref[start - cut:stop - cut, cols] - term

    return rows, cols


def solve_chunk(rest, chunk, sides, *refs):
    outs, ins = refs[-sides:], refs[:-sides]
    first_ref, last_ref, row_ref, cores_ref, *others = ins
    _, core = place(rest)
    for side, out_ref in enumerate(outs):
        k_ref, w_ref, far_ref = others[3 * side:3 * side + 3]
        index = core if side == 0 else 1 - core
        rows, _ = solved(
            rest, chunk, index, first_ref, last_ref, row_ref, k_ref, w_ref, far_ref, cores_ref
        )
        cut, total = first_ref.shape[0], out_ref.shape[0]
        out_ref[:cut] = rows(0, cut)
        out_ref[cut:] = rows(cut, total)


def solve_last(rest, pieces, first_ref, last_ref, row_ref, cores_ref, k_ref, w_ref, far_ref, *refs):
    done_refs, (out_ref, other_ref, sems) = refs[:-3], refs[-3:]
    _, core = place(rest)
    total, width = other_ref.shape
    copies = []
    chunks = out_ref.shape[1] // (2 * width)
    for i, ref in enumerate(done_refs):
        chunk, side = i // 2, i % 2
        index = core if side == 0 else 1 - core
        cols = block(index * chunks + chunk, width)
        copies.append(pltpu.make_async_copy(ref, out_ref.at[:, cols], sems.at[i]))
        copies[-1].start()
    rows, cols = solved(
        rest, chunks - 1, 1 - core, first_ref, last_ref, row_ref, k_ref, w_ref, far_ref, cores_ref
    )
    step = total // pieces
    for i in range(pieces):
        part = slice(i * step, (i + 1) * step)
        other_ref[part] = rows(i * step, (i + 1) * step)
        copy = pltpu.make_async_copy(
            other_ref.at[part], out_ref.at[part, cols], sems.at[len(done_refs) + i]
        )
        copy.start()
        copies.append(copy)
    for copy in copies:
        copy.wait()


def tie(x, *others):
    def body(x_ref, *refs):
        refs[-1][...] = x_ref[...]

    return call(body, shape(*x.shape), (x, *others), 0)


def after(x, *others):
    return lax.optimization_barrier((x, *others))[0]


def swap_wide(x, bit):
    count = lax.axis_size("wide")
    return lax.ppermute(x, "wide", [(w, w ^ (1 << bit)) for w in range(count)])


def swap_narrow(x):
    return lax.ppermute(x, "narrow", [(0, 1), (1, 0)])


def swap_crossed(x, first, second):
    wides, cores = lax.axis_size("wide"), lax.axis_size("narrow")
    route = []
    for w in range(wides):
        for n in range(cores):
            bit = first if n == 0 else second
            route.append((w * cores + n, (w ^ (1 << bit)) * cores + n))
    return lax.ppermute(x, ("wide", "narrow"), route)


def shards(right_side, leaf_inverse, row_bases, dual_bases, woodbury_cores):
    levels, rows, rank = row_bases.shape
    cols = right_side.shape[1]
    half = cols // 2
    rest = lax.axis_size("wide").bit_length() - 1 - levels
    bit3, bit2, bit1 = rest, rest + 1, rest + 2
    cut = rows * 3 // 4

    pairs, last = call(
        base_products, (shape(2 * rank, rank), shape(rank, rank)), tuple(pltpu.with_memory_space_constraint(x, pltpu.HBM) for x in (dual_bases, row_bases)),
        30 * rows * rows * cols, in_specs=[pl.BlockSpec(memory_space=pltpu.HBM)] * 2,
        scratch=[pltpu.VMEM((2, rows, rank), F32)] * 2 + [pltpu.SemaphoreType.DMA((4,))],
    )
    for bit in range(rest):
        pairs, last = pairs + swap_wide(pairs, bit), last + swap_wide(last, bit)
    last_x, pairs_x = swap_wide(last, bit3), swap_wide(pairs, bit3)

    first_rows = call(
        functools.partial(leaf_rows, 0), shape(cut, cols), (leaf_inverse, after(right_side, last)),
        6 * cut * rows * cols,
    )
    last_z = swap_wide(last + last_x, bit2)
    last_rows = call(
        functools.partial(leaf_rows, cut), shape(rows - cut, cols), (leaf_inverse, after(right_side, last_x)),
        6 * (rows - cut) * rows * cols,
    )
    keep, send = call(
        functools.partial(projections, rest), (shape(levels * rank, half),) * 2,
        (dual_bases, first_rows, last_rows), 6 * levels * rank * rows * cols,
        scratch=[pltpu.VMEM((levels * rank, rows), BF16)] * 2,
    )
    recv = swap_narrow(after(send, last_z, pairs_x))
    fix = call(
        functools.partial(corrections, rest), shape(levels * rank, rank),
        (pairs, pairs_x, last, last_x, last_z, woodbury_cores), 36 * rank**3,
    )
    fix_other = swap_narrow(fix)
    if rest:
        keep = keep + recv
        for bit in range(rest):
            keep = keep + swap_wide(keep, bit)
        recv = jnp.zeros_like(keep)
    chunks = 1
    width = half // chunks
    *w, v, q = call(
        corrected, (shape(rank, width),) * chunks + (shape(rank, half),) * 2,
        (keep, recv, fix, fix_other), 18 * rank * rank * half,
    )

    v = tie(v, w[0])
    v_x = swap_wide(v, bit3)
    w = w_mid = [x + swap_crossed(x, bit2, bit3) for x in w]
    q = tie(q, w_mid[0])
    q_x = swap_wide(q, bit3)
    v = v + after(v_x, w_mid[-1])
    w = [x + after(swap_crossed(x, bit3, bit2), v, q) for x in w]
    v_z = swap_wide(v, bit2)
    far = [swap_wide(x, bit1) for x in w]
    w_other = [swap_narrow(after(x, v_z, q_x)) for x in w]
    far_other = [swap_narrow(x) for x in far]
    k = call(
        functools.partial(lower_coefficients, rest), shape(2 * rank, half),
        (after(v, w[0]), v_z, q, q_x, woodbury_cores), 0,
    )
    k_other = swap_narrow(k)
    common = (first_rows, last_rows, row_bases, woodbury_cores)
    done = []
    for i in range(chunks):
        sides = 2 if i < chunks - 1 else 1
        args = (k, w[i], far[i], k_other, w_other[i], far_other[i])[:3 * sides]
        done += call(
            functools.partial(solve_chunk, rest, i, sides), (shape(rows, width),) * sides,
            common + args, 0,
        )
    pieces = 4
    return call(
        functools.partial(solve_last, rest, pieces), shape(rows, cols),
        common + (k_other, w_other[-1], far_other[-1], *done), 0,
        scratch=[pltpu.VMEM((rows, width), F32), pltpu.SemaphoreType.DMA((len(done) + pieces,))],
        out_specs=pl.BlockSpec(memory_space=pltpu.HBM),
    )


def solution(mesh):
    return jax.shard_map(
        shards,
        mesh=mesh,
        in_specs=(
            P(("parts", "wide", "narrow"), None),
            P(("parts", "wide", "narrow"), None),
            P(None, ("parts", "wide", "narrow"), None),
            P(None, ("parts", "wide", "narrow"), None),
            P("parts", None),
        ),
        out_specs=P(("parts", "wide", "narrow"), None),
        check_vma=False,
    )
```

```python
import functools

import jax
import jax.numpy as jnp
from jax import lax
from jax.experimental import pallas as pl
from jax.experimental.pallas import tpu as pltpu
from jax.sharding import PartitionSpec as P

F32, BF16 = jnp.float32, jnp.bfloat16
VMEM = pl.BlockSpec(memory_space=pltpu.VMEM)


def dot(a, b):
    return jnp.dot(a, b, precision=lax.Precision.HIGH, preferred_element_type=F32)


def dot_t(a, b):
    return lax.dot_general(
        a, b, (((0,), (0,)), ((), ())), precision=lax.Precision.HIGH, preferred_element_type=F32
    )


def halves(x):
    high = x.astype(BF16)
    return high, (x - high.astype(F32)).astype(BF16)


def dot3(a, b):
    def one(x, y):
        return jnp.dot(x, y, preferred_element_type=F32)

    return one(a[0], b[0]) + one(a[0], b[1]) + one(a[1], b[0])


def shape(*dims, dtype=F32):
    return jax.ShapeDtypeStruct(dims, dtype)


def call(body, outs, args, flops, in_specs=None, scratch=(), aliases=None, out_specs=None):
    bytes_accessed = sum(a.size * a.dtype.itemsize for a in args)
    return pl.pallas_call(
        body,
        in_specs=in_specs or [VMEM] * len(args),
        out_specs=jax.tree.map(lambda _: VMEM, outs) if out_specs is None else out_specs,
        out_shape=outs,
        scratch_shapes=list(scratch),
        input_output_aliases=aliases or {},
        compiler_params=pltpu.CompilerParams(vmem_limit_bytes=24 * 2**20),
        cost_estimate=pl.CostEstimate(
            flops=flops, bytes_accessed=0, transcendentals=0
        ),
    )(*args)


def place(rest):
    child = lax.shift_right_logical(lax.axis_index("wide"), rest)
    return child, lax.axis_index("narrow")


def block(index, size):
    return pl.ds(pl.multiple_of(index * size, size), size)


def last_product(dual_hbm, row_hbm, out_ref, dual_ref, row_ref, sems):
    rows = dual_ref.shape[0]
    pieces = sems.shape[0]
    step = rows // pieces
    copies = []
    for i in range(pieces):
        part = pl.ds(i * step, step)
        copies.append((
            pltpu.make_async_copy(dual_hbm.at[0, part], dual_ref.at[part], sems.at[i, 0]),
            pltpu.make_async_copy(row_hbm.at[1, part], row_ref.at[part], sems.at[i, 1]),
        ))
        for copy in copies[-1]:
            copy.start()
    total = jnp.zeros(out_ref.shape, F32)
    for i in range(pieces):
        for copy in copies[i]:
            copy.wait()
        part = slice(i * step, (i + 1) * step)
        total += dot_t(dual_ref[part], row_ref[part])
    out_ref[...] = total


def pair_products(dual_ref, row_ref, last_ref, out_ref):
    rank = row_ref.shape[2]
    out_ref[:rank] = dot_t(dual_ref[1], row_ref[2])
    out_ref[rank:] = dot_t(dual_ref[0], row_ref[2])


def leaf_rows(start, leaf_ref, right_ref, field_ref):
    rows = field_ref.shape[0]
    step = min(256, rows)
    right = halves(right_ref[...])
    for i in range(0, rows, step):
        field_ref[i:i + step] = dot3(halves(leaf_ref[start + i:start + i + step]), right)


def projections(rest, dual_ref, first_ref, last_ref, keep_ref, send_ref, high_ref, low_ref):
    levels, rows, rank = dual_ref.shape
    for l in range(levels):
        high, low = halves(dual_ref[l].T)
        high_ref[l * rank:(l + 1) * rank] = high
        low_ref[l * rank:(l + 1) * rank] = low
    _, core = place(rest)
    half = keep_ref.shape[1]
    cut = first_ref.shape[0]
    for out, index in ((keep_ref, core), (send_ref, 1 - core)):
        cols = block(index, half)
        top, bottom = halves(first_ref[:, cols]), halves(last_ref[:, cols])
        out[...] = dot3((high_ref[:, :cut], low_ref[:, :cut]), top) + dot3(
            (high_ref[:, cut:], low_ref[:, cut:]), bottom
        )


def corrections(rest, pairs_ref, pairs_x_ref, last_ref, last_x_ref, last_z_ref, cores_ref, out_ref):
    rank = last_ref.shape[0]
    child, _ = place(rest)
    pair = lax.shift_right_logical(child, 1)
    slot3, slot2 = child & 1, pair & 1
    own = cores_ref[block(6 + child, rank), block(slot3, rank)]
    other = cores_ref[block(6 + (child ^ 1), rank), block(slot3, rank)]
    out_ref[:2 * rank] = dot(pairs_ref[...], own) + dot(pairs_x_ref[...], other)
    own = cores_ref[block(2 + pair, rank), block(slot2, rank)]
    other = cores_ref[block(2 + (pair ^ 1), rank), block(slot2, rank)]
    out_ref[2 * rank:] = dot(last_ref[...] + last_x_ref[...], own) + dot(last_z_ref[...], other)


def corrected(keep_ref, recv_ref, fix_ref, fix_other_ref, w_ref, v_ref, q_ref):
    rank = v_ref.shape[0]
    q = keep_ref[...] + recv_ref[...]
    fix = fix_ref[...] + fix_other_ref[...]
    q1, q2, q3 = q[:rank], q[rank:2 * rank], q[2 * rank:]
    both = dot(fix[:2 * rank], q3)
    v = q2 - both[:rank]
    w_ref[...] = q1 - both[rank:] - dot(fix[2 * rank:], v)
    v_ref[...] = v
    q_ref[...] = q3


def coefficient(level, child, cores_ref, own, other):
    rank = own.shape[0]
    slot = child & 1
    rows = block(2**level - 2 + child, rank)
    return dot(cores_ref[rows, block(slot, rank)], own) + dot(
        cores_ref[rows, block(1 - slot, rank)], other
    )


def lower_two(rest, v_ref, vz_ref, cores_ref, first_ref, last_ref, row_ref, k_ref, out_ref):
    child, core = place(rest)
    k = coefficient(2, lax.shift_right_logical(child, 1), cores_ref, v_ref[...], vz_ref[...])
    k_ref[...] = k
    cols = block(core, k.shape[1])
    cut = first_ref.shape[0]
    term = dot(row_ref[1], k)
    out_ref[:cut] = first_ref[:, cols] - term[:cut]
    out_ref[cut:] = last_ref[:, cols] - term[cut:]


def lower_three(rest, q_ref, qx_ref, cores_ref, field_ref, row_ref, k_ref, out_ref):
    child, _ = place(rest)
    k = coefficient(3, child, cores_ref, q_ref[...], qx_ref[...])
    k_ref[...] = k
    out_ref[...] = field_ref[...] - dot(row_ref[2], k)


def lower_update(index, first_ref, last_ref, row_ref, k, out_ref):
    cols = block(index, k.shape[1])
    cut = first_ref.shape[0]
    lefts = jnp.concatenate([row_ref[1], row_ref[2]], 1)
    term = dot(lefts, k)
    out_ref[:cut] = first_ref[:, cols] - term[:cut]
    out_ref[cut:] = last_ref[:, cols] - term[cut:]


def top_coefficient(rest, w_ref, far_ref, cores_ref):
    rank = w_ref.shape[0]
    child, _ = place(rest)
    slot1 = lax.shift_right_logical(child, 2)
    rows1 = block(slot1, rank)
    return dot(cores_ref[rows1, block(slot1, rank)], w_ref[...]) + dot(
        cores_ref[rows1, block(1 - slot1, rank)], far_ref[...]
    )


def solve_own(rest, own_ref, first_ref, last_ref, row_ref, cores_ref, w_ref, far_ref, *refs):
    *k_refs, out_ref, other_ref = refs
    _, core = place(rest)
    out_ref[...] = own_ref[...] - dot(row_ref[0], top_coefficient(rest, w_ref, far_ref, cores_ref))
    k = jnp.concatenate([ref[...] for ref in k_refs], 0)
    lower_update(1 - core, first_ref, last_ref, row_ref, k, other_ref)


def solve_other(rest, pieces, own_ref, less_ref, row_ref, cores_ref, w_ref, far_ref, out_ref, other_ref, sems):
    _, core = place(rest)
    total, half = own_ref.shape
    mine, theirs = block(core, half), block(1 - core, half)
    copies = [pltpu.make_async_copy(own_ref, out_ref.at[:, mine], sems.at[pieces])]
    copies[0].start()
    top = top_coefficient(rest, w_ref, far_ref, cores_ref)
    step = total // pieces
    for i in range(pieces):
        part = slice(i * step, (i + 1) * step)
        other_ref[part] = less_ref[part] - dot(row_ref[0, part], top)
        copy = pltpu.make_async_copy(other_ref.at[part], out_ref.at[part, theirs], sems.at[i])
        copy.start()
        copies.append(copy)
    for copy in copies:
        copy.wait()


def tie(x, *others):
    def body(x_ref, *refs):
        refs[-1][...] = x_ref[...]

    return call(body, shape(*x.shape), (x, *others), 0)


def after(x, *others):
    return lax.optimization_barrier((x, *others))[0]


def swap_wide(x, bit):
    count = lax.axis_size("wide")
    return lax.ppermute(x, "wide", [(w, w ^ (1 << bit)) for w in range(count)])


def swap_narrow(x):
    return lax.ppermute(x, "narrow", [(0, 1), (1, 0)])


def swap_crossed(x, first, second):
    wides, cores = lax.axis_size("wide"), lax.axis_size("narrow")
    route = []
    for w in range(wides):
        for n in range(cores):
            bit = first if n == 0 else second
            route.append((w * cores + n, (w ^ (1 << bit)) * cores + n))
    return lax.ppermute(x, ("wide", "narrow"), route)


def shards(right_side, leaf_inverse, row_bases, dual_bases, woodbury_cores):
    levels, rows, rank = row_bases.shape
    cols = right_side.shape[1]
    half = cols // 2
    rest = lax.axis_size("wide").bit_length() - 1 - levels
    bit3, bit2, bit1 = rest, rest + 1, rest + 2
    cut = rows // 2

    pieces = 1
    last = call(
        last_product, shape(rank, rank),
        tuple(pltpu.with_memory_space_constraint(x, pltpu.HBM) for x in (dual_bases, row_bases)),
        30 * rows * rows * cols, in_specs=[pl.BlockSpec(memory_space=pltpu.HBM)] * 2,
        scratch=[pltpu.VMEM((rows, rank), F32)] * 2 + [pltpu.SemaphoreType.DMA((pieces, 2))],
    )
    pairs = call(
        pair_products, shape(2 * rank, rank), (dual_bases, row_bases, last), 4 * rows * rank * rank,
    )
    for bit in range(rest):
        pairs, last = pairs + swap_wide(pairs, bit), last + swap_wide(last, bit)
    last_x, pairs_x = swap_wide(last, bit3), swap_wide(pairs, bit3)

    first_rows = call(
        functools.partial(leaf_rows, 0), shape(cut, cols), (leaf_inverse, after(right_side, last)),
        6 * cut * rows * cols,
    )
    last_z = swap_wide(last + last_x, bit2)
    last_rows = call(
        functools.partial(leaf_rows, cut), shape(rows - cut, cols), (leaf_inverse, after(right_side, last_x)),
        6 * (rows - cut) * rows * cols,
    )
    keep, send = call(
        functools.partial(projections, rest), (shape(levels * rank, half),) * 2,
        (dual_bases, first_rows, last_rows), 6 * levels * rank * rows * cols,
        scratch=[pltpu.VMEM((levels * rank, rows), BF16)] * 2,
    )
    recv = swap_narrow(after(send, last_z, pairs_x))
    fix = call(
        functools.partial(corrections, rest), shape(levels * rank, rank),
        (pairs, pairs_x, last, last_x, last_z, woodbury_cores), 36 * rank**3,
    )
    fix_other = swap_narrow(fix)
    if rest:
        keep = keep + recv
        for bit in range(rest):
            keep = keep + swap_wide(keep, bit)
        recv = jnp.zeros_like(keep)
    w, v, q = call(
        corrected, (shape(rank, half),) * 3, (keep, recv, fix, fix_other), 18 * rank * rank * half
    )

    v = tie(v, w)
    v_x = swap_wide(v, bit3)
    w = w_mid = w + swap_crossed(w, bit2, bit3)
    q = tie(q, w_mid)
    q_x = swap_wide(q, bit3)
    v = v + after(v_x, w_mid)
    v_z = swap_wide(v, bit2)
    w = w + after(swap_crossed(w, bit3, bit2), v, q)
    far = swap_wide(w, bit1)
    k2, lower = call(
        functools.partial(lower_two, rest), (shape(rank, half), shape(rows, half)),
        (after(v, w), v_z, woodbury_cores, first_rows, last_rows, row_bases), 0,
    )
    k3, lower = call(
        functools.partial(lower_three, rest), (shape(rank, half), shape(rows, half)),
        (q, q_x, woodbury_cores, lower, row_bases), 0,
    )
    k_other = [swap_narrow(k2), swap_narrow(k3)]
    w_other = swap_narrow(after(w, v_z, q_x))
    far_other = swap_narrow(far)
    own, less = call(
        functools.partial(solve_own, rest), (shape(rows, half),) * 2,
        (lower, first_rows, last_rows, row_bases, woodbury_cores, w, far, *k_other), 0,
    )
    pieces = 4
    return call(
        functools.partial(solve_other, rest, pieces), shape(rows, cols),
        (own, less, row_bases, woodbury_cores, w_other, far_other), 0,
        scratch=[pltpu.VMEM((rows, half), F32), pltpu.SemaphoreType.DMA((pieces + 1,))],
        out_specs=pl.BlockSpec(memory_space=pltpu.HBM),
    )


def solution(mesh):
    return jax.shard_map(
        shards,
        mesh=mesh,
        in_specs=(
            P(("parts", "wide", "narrow"), None),
            P(("parts", "wide", "narrow"), None),
            P(None, ("parts", "wide", "narrow"), None),
            P(None, ("parts", "wide", "narrow"), None),
            P("parts", None),
        ),
        out_specs=P(("parts", "wide", "narrow"), None),
        check_vma=False,
    )
```

```python
import functools

import jax
import jax.numpy as jnp
from jax import lax
from jax.experimental import pallas as pl
from jax.experimental.pallas import tpu as pltpu
from jax.sharding import PartitionSpec as P

F32, BF16 = jnp.float32, jnp.bfloat16
VMEM = pl.BlockSpec(memory_space=pltpu.VMEM)


def dot(a, b):
    return jnp.dot(a, b, precision=lax.Precision.HIGH, preferred_element_type=F32)


def dot_t(a, b):
    return lax.dot_general(
        a, b, (((0,), (0,)), ((), ())), precision=lax.Precision.HIGH, preferred_element_type=F32
    )


def halves(x):
    high = x.astype(BF16)
    return high, (x - high.astype(F32)).astype(BF16)


def dot3(a, b):
    def one(x, y):
        return jnp.dot(x, y, preferred_element_type=F32)

    return one(a[0], b[0]) + one(a[0], b[1]) + one(a[1], b[0])


def shape(*dims, dtype=F32):
    return jax.ShapeDtypeStruct(dims, dtype)


def call(body, outs, args, flops, in_specs=None, scratch=(), aliases=None, out_specs=None):
    bytes_accessed = sum(a.size * a.dtype.itemsize for a in args)
    return pl.pallas_call(
        body,
        in_specs=in_specs or [VMEM] * len(args),
        out_specs=jax.tree.map(lambda _: VMEM, outs) if out_specs is None else out_specs,
        out_shape=outs,
        scratch_shapes=list(scratch),
        input_output_aliases=aliases or {},
        compiler_params=pltpu.CompilerParams(vmem_limit_bytes=24 * 2**20),
        cost_estimate=pl.CostEstimate(
            flops=flops, bytes_accessed=0, transcendentals=0
        ),
    )(*args)


def place(rest):
    child = lax.shift_right_logical(lax.axis_index("wide"), rest)
    return child, lax.axis_index("narrow")


def block(index, size):
    return pl.ds(pl.multiple_of(index * size, size), size)


def last_product(dual_hbm, row_hbm, out_ref, dual_ref, row_ref, sems):
    rows = dual_ref.shape[0]
    pieces = sems.shape[0]
    step = rows // pieces
    copies = []
    for i in range(pieces):
        part = pl.ds(i * step, step)
        copies.append((
            pltpu.make_async_copy(dual_hbm.at[0, part], dual_ref.at[part], sems.at[i, 0]),
            pltpu.make_async_copy(row_hbm.at[1, part], row_ref.at[part], sems.at[i, 1]),
        ))
        for copy in copies[-1]:
            copy.start()
    total = jnp.zeros(out_ref.shape, F32)
    for i in range(pieces):
        for copy in copies[i]:
            copy.wait()
        part = slice(i * step, (i + 1) * step)
        total += dot_t(dual_ref[part], row_ref[part])
    out_ref[...] = total


def pair_products(dual_ref, row_ref, last_ref, out_ref):
    rank = row_ref.shape[2]
    out_ref[:rank] = dot_t(dual_ref[1], row_ref[2])
    out_ref[rank:] = dot_t(dual_ref[0], row_ref[2])


def leaf_rows(start, leaf_ref, right_ref, field_ref):
    rows = field_ref.shape[0]
    step = min(256, rows)
    right = halves(right_ref[...])
    for i in range(0, rows, step):
        field_ref[i:i + step] = dot3(halves(leaf_ref[start + i:start + i + step]), right)


def projections(
    rest, leaf_ref, right_ref, dual_ref, first_ref, last_ref, keep_ref, send_ref, high_ref, low_ref
):
    leaf_rows(first_ref.shape[0], leaf_ref, right_ref, last_ref)
    levels, rows, rank = dual_ref.shape
    for l in range(levels):
        high, low = halves(dual_ref[l].T)
        high_ref[l * rank:(l + 1) * rank] = high
        low_ref[l * rank:(l + 1) * rank] = low
    _, core = place(rest)
    half = keep_ref.shape[1]
    cut = first_ref.shape[0]
    for out, index in ((keep_ref, core), (send_ref, 1 - core)):
        cols = block(index, half)
        top, bottom = halves(first_ref[:, cols]), halves(last_ref[:, cols])
        out[...] = dot3((high_ref[:, :cut], low_ref[:, :cut]), top) + dot3(
            (high_ref[:, cut:], low_ref[:, cut:]), bottom
        )


def pair_corrections(rest, pairs_ref, pairs_x_ref, cores_ref, out_ref):
    rank = pairs_ref.shape[1]
    child, _ = place(rest)
    cols = block(child & 1, rank)
    out_ref[...] = dot(pairs_ref[...], cores_ref[block(6 + child, rank), cols]) + dot(
        pairs_x_ref[...], cores_ref[block(6 + (child ^ 1), rank), cols]
    )


def last_corrections(rest, last_ref, last_x_ref, last_z_ref, cores_ref, out_ref):
    rank = last_ref.shape[0]
    child, _ = place(rest)
    pair = lax.shift_right_logical(child, 1)
    cols = block(pair & 1, rank)
    out_ref[...] = dot(
        last_ref[...] + last_x_ref[...], cores_ref[block(2 + pair, rank), cols]
    ) + dot(last_z_ref[...], cores_ref[block(2 + (pair ^ 1), rank), cols])


def corrected(keep_ref, recv_ref, fix_ref, fix_other_ref, w_ref, v_ref, q_ref):
    rank = v_ref.shape[0]
    q = keep_ref[...] + recv_ref[...]
    q1, q2, q3 = q[:rank], q[rank:2 * rank], q[2 * rank:]
    both = dot(fix_ref[...] + fix_other_ref[...], q3)
    v_ref[...] = q2 - both[:rank]
    w_ref[...] = q1 - both[rank:]
    q_ref[...] = q3


def corrected_top(w_ref, v_ref, fix_ref, fix_other_ref, out_ref):
    out_ref[...] = w_ref[...] - dot(fix_ref[...] + fix_other_ref[...], v_ref[...])


def coefficient(level, child, cores_ref, own, other):
    rank = own.shape[0]
    slot = child & 1
    rows = block(2**level - 2 + child, rank)
    return dot(cores_ref[rows, block(slot, rank)], own) + dot(
        cores_ref[rows, block(1 - slot, rank)], other
    )


def top_matrix(rest, row_ref, cores_ref, out_ref):
    rank = row_ref.shape[2]
    child, _ = place(rest)
    both = dot(row_ref[0], cores_ref[block(lax.shift_right_logical(child, 2), rank)])
    out_ref[0] = both[:, :rank]
    out_ref[1] = both[:, rank:]


def lower_two(rest, v_ref, vz_ref, cores_ref, first_ref, last_ref, row_ref, k_ref, out_ref):
    child, core = place(rest)
    k = coefficient(2, lax.shift_right_logical(child, 1), cores_ref, v_ref[...], vz_ref[...])
    k_ref[...] = k
    cols = block(core, k.shape[1])
    cut = first_ref.shape[0]
    term = dot(row_ref[1], k)
    out_ref[:cut] = first_ref[:, cols] - term[:cut]
    out_ref[cut:] = last_ref[:, cols] - term[cut:]


def lower_three(rest, q_ref, qx_ref, cores_ref, field_ref, row_ref, top_ref, w_ref, k_ref, out_ref):
    child, _ = place(rest)
    side = lax.shift_right_logical(child, 2)
    k = coefficient(3, child, cores_ref, q_ref[...], qx_ref[...])
    k_ref[...] = k
    lefts = jnp.concatenate([row_ref[2], top_ref[side]], 1)
    out_ref[...] = field_ref[...] - dot(lefts, jnp.concatenate([k, w_ref[...]], 0))


def solve_own(rest, own_ref, first_ref, last_ref, row_ref, top_ref, far_ref, w_ref, *refs):
    *k_refs, out_ref, other_ref = refs
    child, core = place(rest)
    side = lax.shift_right_logical(child, 2)
    out_ref[...] = own_ref[...] - dot(top_ref[1 - side], far_ref[...])
    cols = block(1 - core, w_ref.shape[1])
    cut = first_ref.shape[0]
    lefts = jnp.concatenate([row_ref[1], row_ref[2], top_ref[side]], 1)
    term = dot(lefts, jnp.concatenate([ref[...] for ref in (*k_refs, w_ref)], 0))
    other_ref[:cut] = first_ref[:, cols] - term[:cut]
    other_ref[cut:] = last_ref[:, cols] - term[cut:]


def solve_other(rest, pieces, own_ref, less_ref, top_ref, far_ref, out_ref, other_ref, sems):
    child, core = place(rest)
    side = lax.shift_right_logical(child, 2)
    total, half = own_ref.shape
    mine, theirs = block(core, half), block(1 - core, half)
    copies = [pltpu.make_async_copy(own_ref, out_ref.at[:, mine], sems.at[pieces])]
    copies[0].start()
    step = total // pieces
    for i in range(pieces):
        part = slice(i * step, (i + 1) * step)
        other_ref[part] = less_ref[part] - dot(top_ref[1 - side, part], far_ref[...])
        copy = pltpu.make_async_copy(other_ref.at[part], out_ref.at[part, theirs], sems.at[i])
        copy.start()
        copies.append(copy)
    for copy in copies:
        copy.wait()


def tie(x, *others):
    def body(x_ref, *refs):
        refs[-1][...] = x_ref[...]

    return call(body, shape(*x.shape), (x, *others), 0)


def after(x, *others):
    return lax.optimization_barrier((x, *others))[0]


def swap_wide(x, bit):
    count = lax.axis_size("wide")
    return lax.ppermute(x, "wide", [(w, w ^ (1 << bit)) for w in range(count)])


def swap_narrow(x):
    return lax.ppermute(x, "narrow", [(0, 1), (1, 0)])


def swap_crossed(x, first, second, other_core=False):
    wides, cores = lax.axis_size("wide"), lax.axis_size("narrow")
    route = []
    for w in range(wides):
        for n in range(cores):
            bit = first if n == 0 else second
            route.append((w * cores + n, (w ^ (1 << bit)) * cores + (n ^ other_core)))
    return lax.ppermute(x, ("wide", "narrow"), route)


def swap_diagonal(x, bit):
    return swap_crossed(x, bit, bit, True)


def shards(right_side, leaf_inverse, row_bases, dual_bases, woodbury_cores):
    levels, rows, rank = row_bases.shape
    cols = right_side.shape[1]
    half = cols // 2
    rest = lax.axis_size("wide").bit_length() - 1 - levels
    bit3, bit2, bit1 = rest, rest + 1, rest + 2
    cut = rows // 2

    pieces = 1
    last = call(
        last_product, shape(rank, rank),
        tuple(pltpu.with_memory_space_constraint(x, pltpu.HBM) for x in (dual_bases, row_bases)),
        30 * rows * rows * cols, in_specs=[pl.BlockSpec(memory_space=pltpu.HBM)] * 2,
        scratch=[pltpu.VMEM((rows, rank), F32)] * 2 + [pltpu.SemaphoreType.DMA((pieces, 2))],
    )
    pairs = call(
        pair_products, shape(2 * rank, rank), (dual_bases, row_bases, last), 4 * rows * rank * rank,
    )
    for bit in range(rest):
        pairs, last = pairs + swap_wide(pairs, bit), last + swap_wide(last, bit)
    last_x, pairs_x = swap_diagonal(last, bit3), swap_diagonal(pairs, bit3)

    first_rows = call(
        functools.partial(leaf_rows, 0), shape(cut, cols), (leaf_inverse, after(right_side, last)),
        6 * cut * rows * cols,
    )
    last_z = swap_diagonal(last + after(last_x, first_rows), bit2)
    last_rows, keep, send = call(
        functools.partial(projections, rest),
        (shape(rows - cut, cols),) + (shape(levels * rank, half),) * 2,
        (leaf_inverse, after(right_side, last_x), dual_bases, first_rows), 0,
        scratch=[pltpu.VMEM((levels * rank, rows), BF16)] * 2,
    )
    fix = call(
        functools.partial(pair_corrections, rest), shape(2 * rank, rank),
        (pairs, pairs_x, woodbury_cores), 0,
    )
    recv = swap_narrow(after(send, last_z, fix))
    fix_other = swap_narrow(after(fix, last_z))
    fix_top = call(
        functools.partial(last_corrections, rest), shape(rank, rank),
        (last, last_x, last_z, woodbury_cores), 0,
    )
    fix_top_other = swap_narrow(after(fix_top, fix))
    if rest:
        keep = keep + recv
        for bit in range(rest):
            keep = keep + swap_wide(keep, bit)
        recv = jnp.zeros_like(keep)
    w, v, q = call(
        corrected, (shape(rank, half),) * 3, (keep, recv, fix, fix_other), 18 * rank * rank * half
    )
    w = call(corrected_top, shape(rank, half), (w, v, fix_top, fix_top_other), 0)

    v = tie(v, w)
    v_x = swap_wide(v, bit3)
    top = call(
        functools.partial(top_matrix, rest), shape(2, rows, rank),
        (row_bases, after(woodbury_cores, w)), 0,
    )
    w = w_mid = w + after(swap_crossed(w, bit2, bit3), top)
    q = tie(q, w_mid)
    q_x = swap_wide(q, bit3)
    v = v + after(v_x, w_mid)
    v_z = swap_wide(v, bit2)
    w = w + after(swap_crossed(w, bit3, bit2), v, q)
    far = swap_wide(w, bit1)
    k2, lower = call(
        functools.partial(lower_two, rest), (shape(rank, half), shape(rows, half)),
        (after(v, w), v_z, woodbury_cores, first_rows, last_rows, row_bases), 0,
    )
    k3, lower = call(
        functools.partial(lower_three, rest), (shape(rank, half), shape(rows, half)),
        (q, q_x, woodbury_cores, lower, row_bases, top, w), 0,
    )
    k_other = [swap_narrow(k2), swap_narrow(k3)]
    w_other = swap_narrow(after(w, k2))
    far_other = swap_narrow(far)
    own, less = call(
        functools.partial(solve_own, rest), (shape(rows, half),) * 2,
        (lower, first_rows, last_rows, row_bases, top, far, w_other, *k_other), 0,
    )
    pieces = 4
    return call(
        functools.partial(solve_other, rest, pieces), shape(rows, cols),
        (own, less, top, far_other), 0,
        scratch=[pltpu.VMEM((rows, half), F32), pltpu.SemaphoreType.DMA((pieces + 1,))],
        out_specs=pl.BlockSpec(memory_space=pltpu.HBM),
    )


def solution(mesh):
    return jax.shard_map(
        shards,
        mesh=mesh,
        in_specs=(
            P(("parts", "wide", "narrow"), None),
            P(("parts", "wide", "narrow"), None),
            P(None, ("parts", "wide", "narrow"), None),
            P(None, ("parts", "wide", "narrow"), None),
            P("parts", None),
        ),
        out_specs=P(("parts", "wide", "narrow"), None),
        check_vma=False,
    )
```

```python
import functools

import jax
import jax.numpy as jnp
from jax import lax
from jax.experimental import pallas as pl
from jax.experimental.pallas import tpu as pltpu
from jax.sharding import PartitionSpec as P

F32, BF16 = jnp.float32, jnp.bfloat16
VMEM = pl.BlockSpec(memory_space=pltpu.VMEM)


def dot(a, b):
    return jnp.dot(a, b, precision=lax.Precision.HIGH, preferred_element_type=F32)


def dot_t(a, b):
    return lax.dot_general(
        a, b, (((0,), (0,)), ((), ())), precision=lax.Precision.HIGH, preferred_element_type=F32
    )


def halves(x):
    high = x.astype(BF16)
    return high, (x - high.astype(F32)).astype(BF16)


def dot3(a, b):
    def one(x, y):
        return jnp.dot(x, y, preferred_element_type=F32)

    return one(a[0], b[0]) + one(a[0], b[1]) + one(a[1], b[0])


def shape(*dims, dtype=F32):
    return jax.ShapeDtypeStruct(dims, dtype)


def call(body, outs, args, flops, in_specs=None, scratch=(), aliases=None, out_specs=None):
    bytes_accessed = sum(a.size * a.dtype.itemsize for a in args)
    return pl.pallas_call(
        body,
        in_specs=in_specs or [VMEM] * len(args),
        out_specs=jax.tree.map(lambda _: VMEM, outs) if out_specs is None else out_specs,
        out_shape=outs,
        scratch_shapes=list(scratch),
        input_output_aliases=aliases or {},
        compiler_params=pltpu.CompilerParams(vmem_limit_bytes=24 * 2**20),
        cost_estimate=pl.CostEstimate(
            flops=flops, bytes_accessed=0, transcendentals=0
        ),
    )(*args)


def place(rest):
    child = lax.shift_right_logical(lax.axis_index("wide"), rest)
    return child, lax.axis_index("narrow")


def block(index, size):
    return pl.ds(pl.multiple_of(index * size, size), size)


def last_product(dual_hbm, row_hbm, out_ref, dual_ref, row_ref, sems):
    rows = dual_ref.shape[0]
    pieces = sems.shape[0]
    step = rows // pieces
    copies = []
    for i in range(pieces):
        part = pl.ds(i * step, step)
        copies.append((
            pltpu.make_async_copy(dual_hbm.at[0, part], dual_ref.at[part], sems.at[i, 0]),
            pltpu.make_async_copy(row_hbm.at[1, part], row_ref.at[part], sems.at[i, 1]),
        ))
        for copy in copies[-1]:
            copy.start()
    total = jnp.zeros(out_ref.shape, F32)
    for i in range(pieces):
        for copy in copies[i]:
            copy.wait()
        part = slice(i * step, (i + 1) * step)
        total += dot_t(dual_ref[part], row_ref[part])
    out_ref[...] = total


def pair_products(dual_ref, row_ref, last_ref, out_ref):
    rank = row_ref.shape[2]
    out_ref[:rank] = dot_t(dual_ref[1], row_ref[2])
    out_ref[rank:] = dot_t(dual_ref[0], row_ref[2])


def leaf_rows(start, leaf_ref, right_ref, field_ref):
    rows = field_ref.shape[0]
    step = min(256, rows)
    right = halves(right_ref[...])
    for i in range(0, rows, step):
        field_ref[i:i + step] = dot3(halves(leaf_ref[start + i:start + i + step]), right)


def projections(
    rest, leaf_ref, right_ref, dual_ref, first_ref, last_ref, keep_ref, send_ref, high_ref, low_ref
):
    leaf_rows(first_ref.shape[0], leaf_ref, right_ref, last_ref)
    levels, rows, rank = dual_ref.shape
    for l in range(levels):
        high, low = halves(dual_ref[l].T)
        high_ref[l * rank:(l + 1) * rank] = high
        low_ref[l * rank:(l + 1) * rank] = low
    _, core = place(rest)
    half = keep_ref.shape[1]
    cut = first_ref.shape[0]
    for out, index in ((keep_ref, core), (send_ref, 1 - core)):
        cols = block(index, half)
        top, bottom = halves(first_ref[:, cols]), halves(last_ref[:, cols])
        out[...] = dot3((high_ref[:, :cut], low_ref[:, :cut]), top) + dot3(
            (high_ref[:, cut:], low_ref[:, cut:]), bottom
        )


def pair_corrections(rest, pairs_ref, pairs_x_ref, cores_ref, out_ref):
    rank = pairs_ref.shape[1]
    child, _ = place(rest)
    cols = block(child & 1, rank)
    out_ref[...] = dot(pairs_ref[...], cores_ref[block(6 + child, rank), cols]) + dot(
        pairs_x_ref[...], cores_ref[block(6 + (child ^ 1), rank), cols]
    )


def last_corrections(rest, last_ref, last_x_ref, last_z_ref, cores_ref, out_ref):
    rank = last_ref.shape[0]
    child, _ = place(rest)
    pair = lax.shift_right_logical(child, 1)
    cols = block(pair & 1, rank)
    out_ref[...] = dot(
        last_ref[...] + last_x_ref[...], cores_ref[block(2 + pair, rank), cols]
    ) + dot(last_z_ref[...], cores_ref[block(2 + (pair ^ 1), rank), cols])


def corrected(keep_ref, recv_ref, fix_ref, fix_other_ref, w_ref, v_ref, q_ref):
    rank = v_ref.shape[0]
    q = keep_ref[...] + recv_ref[...]
    q1, q2, q3 = q[:rank], q[rank:2 * rank], q[2 * rank:]
    both = dot(fix_ref[...] + fix_other_ref[...], q3)
    v_ref[...] = q2 - both[:rank]
    w_ref[...] = q1 - both[rank:]
    q_ref[...] = q3


def corrected_top(w_ref, v_ref, fix_ref, fix_other_ref, out_ref):
    out_ref[...] = w_ref[...] - dot(fix_ref[...] + fix_other_ref[...], v_ref[...])


def coefficient(level, child, cores_ref, own, other):
    rank = own.shape[0]
    slot = child & 1
    rows = block(2**level - 2 + child, rank)
    return dot(cores_ref[rows, block(slot, rank)], own) + dot(
        cores_ref[rows, block(1 - slot, rank)], other
    )


def top_matrix(rest, row_ref, cores_ref, out_ref):
    rank = row_ref.shape[2]
    child, _ = place(rest)
    both = dot(row_ref[0], cores_ref[block(lax.shift_right_logical(child, 2), rank)])
    out_ref[0] = both[:, :rank]
    out_ref[1] = both[:, rank:]


def lower_two(rest, v_ref, vz_ref, cores_ref, first_ref, last_ref, row_ref, k_ref, out_ref):
    child, core = place(rest)
    k = coefficient(2, lax.shift_right_logical(child, 1), cores_ref, v_ref[...], vz_ref[...])
    k_ref[...] = k
    cols = block(core, k.shape[1])
    cut = first_ref.shape[0]
    term = dot(row_ref[1], k)
    out_ref[:cut] = first_ref[:, cols] - term[:cut]
    out_ref[cut:] = last_ref[:, cols] - term[cut:]


def lower_three(rest, q_ref, qx_ref, cores_ref, field_ref, row_ref, top_ref, w_ref, k_ref, out_ref):
    child, _ = place(rest)
    side = lax.shift_right_logical(child, 2)
    k = coefficient(3, child, cores_ref, q_ref[...], qx_ref[...])
    k_ref[...] = k
    lefts = jnp.concatenate([row_ref[2], top_ref[side]], 1)
    out_ref[...] = field_ref[...] - dot(lefts, jnp.concatenate([k, w_ref[...]], 0))


def solve_own(rest, own_ref, first_ref, last_ref, row_ref, top_ref, far_ref, *refs):
    *k_refs, out_ref, other_ref = refs
    child, core = place(rest)
    side = lax.shift_right_logical(child, 2)
    out_ref[...] = own_ref[...] - dot(top_ref[1 - side], far_ref[...])
    cols = block(1 - core, far_ref.shape[1])
    cut = first_ref.shape[0]
    lefts = jnp.concatenate([row_ref[1], row_ref[2]], 1)
    term = dot(lefts, jnp.concatenate([ref[...] for ref in k_refs], 0))
    other_ref[:cut] = first_ref[:, cols] - term[:cut]
    other_ref[cut:] = last_ref[:, cols] - term[cut:]


def solve_other(rest, pieces, own_ref, less_ref, top_ref, w_ref, far_ref, out_ref, other_ref, sems):
    child, core = place(rest)
    side = lax.shift_right_logical(child, 2)
    total, half = own_ref.shape
    mine, theirs = block(core, half), block(1 - core, half)
    copies = [pltpu.make_async_copy(own_ref, out_ref.at[:, mine], sems.at[pieces])]
    copies[0].start()
    both = jnp.concatenate([w_ref[...], far_ref[...]], 0)
    step = total // pieces
    for i in range(pieces):
        part = slice(i * step, (i + 1) * step)
        lefts = jnp.concatenate([top_ref[side, part], top_ref[1 - side, part]], 1)
        other_ref[part] = less_ref[part] - dot(lefts, both)
        copy = pltpu.make_async_copy(other_ref.at[part], out_ref.at[part, theirs], sems.at[i])
        copy.start()
        copies.append(copy)
    for copy in copies:
        copy.wait()


def tie(x, *others):
    def body(x_ref, *refs):
        refs[-1][...] = x_ref[...]

    return call(body, shape(*x.shape), (x, *others), 0)


def after(x, *others):
    return lax.optimization_barrier((x, *others))[0]


def swap_wide(x, bit):
    count = lax.axis_size("wide")
    return lax.ppermute(x, "wide", [(w, w ^ (1 << bit)) for w in range(count)])


def swap_narrow(x):
    return lax.ppermute(x, "narrow", [(0, 1), (1, 0)])


def swap_crossed(x, first, second, other_core=False):
    wides, cores = lax.axis_size("wide"), lax.axis_size("narrow")
    route = []
    for w in range(wides):
        for n in range(cores):
            bit = first if n == 0 else second
            route.append((w * cores + n, (w ^ (1 << bit)) * cores + (n ^ other_core)))
    return lax.ppermute(x, ("wide", "narrow"), route)


def swap_diagonal(x, bit):
    return swap_crossed(x, bit, bit, True)


def shards(right_side, leaf_inverse, row_bases, dual_bases, woodbury_cores):
    levels, rows, rank = row_bases.shape
    cols = right_side.shape[1]
    half = cols // 2
    rest = lax.axis_size("wide").bit_length() - 1 - levels
    bit3, bit2, bit1 = rest, rest + 1, rest + 2
    cut = rows // 2

    pieces = 1
    last = call(
        last_product, shape(rank, rank),
        tuple(pltpu.with_memory_space_constraint(x, pltpu.HBM) for x in (dual_bases, row_bases)),
        30 * rows * rows * cols, in_specs=[pl.BlockSpec(memory_space=pltpu.HBM)] * 2,
        scratch=[pltpu.VMEM((rows, rank), F32)] * 2 + [pltpu.SemaphoreType.DMA((pieces, 2))],
    )
    pairs = call(
        pair_products, shape(2 * rank, rank), (dual_bases, row_bases, last), 4 * rows * rank * rank,
    )
    for bit in range(rest):
        pairs, last = pairs + swap_wide(pairs, bit), last + swap_wide(last, bit)
    last_x, pairs_x = swap_diagonal(last, bit3), swap_diagonal(pairs, bit3)

    first_rows = call(
        functools.partial(leaf_rows, 0), shape(cut, cols), (leaf_inverse, after(right_side, last)),
        6 * cut * rows * cols,
    )
    last_z = swap_diagonal(last + after(last_x, first_rows), bit2)
    last_rows, keep, send = call(
        functools.partial(projections, rest),
        (shape(rows - cut, cols),) + (shape(levels * rank, half),) * 2,
        (leaf_inverse, after(right_side, last_x), dual_bases, first_rows), 0,
        scratch=[pltpu.VMEM((levels * rank, rows), BF16)] * 2,
    )
    fix = call(
        functools.partial(pair_corrections, rest), shape(2 * rank, rank),
        (pairs, pairs_x, woodbury_cores), 0,
    )
    recv = swap_narrow(after(send, last_z, fix))
    fix_other = swap_narrow(fix)
    fix_top = call(
        functools.partial(last_corrections, rest), shape(rank, rank),
        (last, last_x, last_z, woodbury_cores), 0,
    )
    fix_top_other = swap_narrow(after(fix_top, fix))
    if rest:
        keep = keep + recv
        for bit in range(rest):
            keep = keep + swap_wide(keep, bit)
        recv = jnp.zeros_like(keep)
    w, v, q = call(
        corrected, (shape(rank, half),) * 3, (keep, recv, fix, fix_other), 18 * rank * rank * half
    )
    w = call(corrected_top, shape(rank, half), (w, v, fix_top, fix_top_other), 0)

    v = tie(v, w)
    v_x = swap_wide(v, bit3)
    top = call(
        functools.partial(top_matrix, rest), shape(2, rows, rank),
        (row_bases, after(woodbury_cores, w)), 0,
    )
    w = w_mid = w + after(swap_crossed(w, bit2, bit3), top, q)
    q = tie(q, top)
    q_x = swap_wide(q, bit3)
    v = v + after(v_x, w_mid)
    v_z = swap_wide(v, bit2)
    w = w + after(swap_crossed(w, bit3, bit2), v)
    far = swap_wide(w, bit1)
    k2, lower = call(
        functools.partial(lower_two, rest), (shape(rank, half), shape(rows, half)),
        (after(v, w), v_z, woodbury_cores, first_rows, last_rows, row_bases), 0,
    )
    k3, lower = call(
        functools.partial(lower_three, rest), (shape(rank, half), shape(rows, half)),
        (q, q_x, woodbury_cores, lower, row_bases, top, w), 0,
    )
    k_other = [swap_narrow(k2), swap_narrow(k3)]
    w_other = swap_narrow(after(w, k2))
    far_other = swap_narrow(far)
    own, less = call(
        functools.partial(solve_own, rest), (shape(rows, half),) * 2,
        (lower, first_rows, last_rows, row_bases, top, far, *k_other), 0,
    )
    pieces = 4
    return call(
        functools.partial(solve_other, rest, pieces), shape(rows, cols),
        (own, less, top, w_other, far_other), 0,
        scratch=[pltpu.VMEM((rows, half), F32), pltpu.SemaphoreType.DMA((pieces + 1,))],
        out_specs=pl.BlockSpec(memory_space=pltpu.HBM),
    )


def solution(mesh):
    return jax.shard_map(
        shards,
        mesh=mesh,
        in_specs=(
            P(("parts", "wide", "narrow"), None),
            P(("parts", "wide", "narrow"), None),
            P(None, ("parts", "wide", "narrow"), None),
            P(None, ("parts", "wide", "narrow"), None),
            P("parts", None),
        ),
        out_specs=P(("parts", "wide", "narrow"), None),
        check_vma=False,
    )
```

```python
import functools

import jax
import jax.numpy as jnp
from jax import lax
from jax.experimental import pallas as pl
from jax.experimental.pallas import tpu as pltpu
from jax.sharding import PartitionSpec as P

F32, BF16 = jnp.float32, jnp.bfloat16
VMEM = pl.BlockSpec(memory_space=pltpu.VMEM)


def halves(x):
    high = x.astype(BF16)
    return high, (x - high.astype(F32)).astype(BF16)


def dot3(a, b, dims=((1,), (0,))):
    def one(x, y):
        return lax.dot_general(x, y, (dims, ((), ())), preferred_element_type=F32)

    return one(a[0], b[0]) + one(a[0], b[1]) + one(a[1], b[0])


def dot(a, b):
    return dot3(halves(a), halves(b))


def dot_t(a, b):
    return dot3(halves(a), halves(b), ((0,), (0,)))


def shape(*dims, dtype=F32):
    return jax.ShapeDtypeStruct(dims, dtype)


def call(body, outs, args, flops, in_specs=None, scratch=(), aliases=None, out_specs=None):
    bytes_accessed = sum(a.size * a.dtype.itemsize for a in args)
    return pl.pallas_call(
        body,
        in_specs=in_specs or [VMEM] * len(args),
        out_specs=jax.tree.map(lambda _: VMEM, outs) if out_specs is None else out_specs,
        out_shape=outs,
        scratch_shapes=list(scratch),
        input_output_aliases=aliases or {},
        compiler_params=pltpu.CompilerParams(vmem_limit_bytes=24 * 2**20),
        cost_estimate=pl.CostEstimate(
            flops=flops, bytes_accessed=0, transcendentals=0
        ),
    )(*args)


def place(rest):
    child = lax.shift_right_logical(lax.axis_index("wide"), rest)
    return child, lax.axis_index("narrow")


def block(index, size):
    return pl.ds(pl.multiple_of(index * size, size), size)


def last_product(dual_hbm, row_hbm, out_ref, dual_ref, row_ref, sems):
    rows = dual_ref.shape[0]
    pieces = sems.shape[0]
    step = rows // pieces
    copies = []
    for i in range(pieces):
        part = pl.ds(i * step, step)
        copies.append((
            pltpu.make_async_copy(dual_hbm.at[0, part], dual_ref.at[part], sems.at[i, 0]),
            pltpu.make_async_copy(row_hbm.at[1, part], row_ref.at[part], sems.at[i, 1]),
        ))
        for copy in copies[-1]:
            copy.start()
    total = jnp.zeros(out_ref.shape, F32)
    for i in range(pieces):
        for copy in copies[i]:
            copy.wait()
        part = slice(i * step, (i + 1) * step)
        total += dot_t(dual_ref[part], row_ref[part])
    out_ref[...] = total


def pair_products(dual_ref, row_ref, last_ref, out_ref):
    rank = row_ref.shape[2]
    out_ref[:rank] = dot_t(dual_ref[1], row_ref[2])
    out_ref[rank:] = dot_t(dual_ref[0], row_ref[2])


def leaf_rows(start, leaf_ref, right_ref, field_ref):
    rows = field_ref.shape[0]
    step = min(256, rows)
    right = halves(right_ref[...])
    for i in range(0, rows, step):
        field_ref[i:i + step] = dot3(halves(leaf_ref[start + i:start + i + step]), right)


def projections(
    rest, leaf_ref, right_ref, dual_ref, first_ref, last_ref, keep_ref, send_ref, high_ref, low_ref
):
    leaf_rows(first_ref.shape[0], leaf_ref, right_ref, last_ref)
    levels, rows, rank = dual_ref.shape
    for l in range(levels):
        high, low = halves(dual_ref[l].T)
        high_ref[l * rank:(l + 1) * rank] = high
        low_ref[l * rank:(l + 1) * rank] = low
    _, core = place(rest)
    half = keep_ref.shape[1]
    cut = first_ref.shape[0]
    for out, index in ((keep_ref, core), (send_ref, 1 - core)):
        cols = block(index, half)
        top, bottom = halves(first_ref[:, cols]), halves(last_ref[:, cols])
        out[...] = dot3((high_ref[:, :cut], low_ref[:, :cut]), top) + dot3(
            (high_ref[:, cut:], low_ref[:, cut:]), bottom
        )


def pair_corrections(rest, pairs_ref, pairs_x_ref, cores_ref, out_ref):
    rank = pairs_ref.shape[1]
    child, _ = place(rest)
    cols = block(child & 1, rank)
    out_ref[...] = dot(pairs_ref[...], cores_ref[block(6 + child, rank), cols]) + dot(
        pairs_x_ref[...], cores_ref[block(6 + (child ^ 1), rank), cols]
    )


def last_corrections(rest, last_ref, last_x_ref, last_z_ref, cores_ref, out_ref):
    rank = last_ref.shape[0]
    child, _ = place(rest)
    pair = lax.shift_right_logical(child, 1)
    cols = block(pair & 1, rank)
    out_ref[...] = dot(
        last_ref[...] + last_x_ref[...], cores_ref[block(2 + pair, rank), cols]
    ) + dot(last_z_ref[...], cores_ref[block(2 + (pair ^ 1), rank), cols])


def corrected(keep_ref, recv_ref, fix_ref, fix_other_ref, w_ref, v_ref, q_ref):
    rank = v_ref.shape[0]
    q = keep_ref[...] + recv_ref[...]
    q1, q2, q3 = q[:rank], q[rank:2 * rank], q[2 * rank:]
    both = dot(fix_ref[...] + fix_other_ref[...], q3)
    v_ref[...] = q2 - both[:rank]
    w_ref[...] = q1 - both[rank:]
    q_ref[...] = q3


def corrected_top(w_ref, v_ref, fix_ref, fix_other_ref, out_ref):
    out_ref[...] = w_ref[...] - dot(fix_ref[...] + fix_other_ref[...], v_ref[...])


def coefficient(level, child, cores_ref, own, other):
    rank = own.shape[0]
    slot = child & 1
    rows = block(2**level - 2 + child, rank)
    return dot(cores_ref[rows, block(slot, rank)], own) + dot(
        cores_ref[rows, block(1 - slot, rank)], other
    )


def top_matrix(rest, row_ref, cores_ref, out_ref):
    rank = row_ref.shape[2]
    child, _ = place(rest)
    both = dot(row_ref[0], cores_ref[block(lax.shift_right_logical(child, 2), rank)])
    out_ref[0] = both[:, :rank]
    out_ref[1] = both[:, rank:]


def lower_two(rest, v_ref, vz_ref, cores_ref, first_ref, last_ref, row_ref, k_ref, out_ref):
    child, core = place(rest)
    k = coefficient(2, lax.shift_right_logical(child, 1), cores_ref, v_ref[...], vz_ref[...])
    k_ref[...] = k
    cols = block(core, k.shape[1])
    cut = first_ref.shape[0]
    term = dot(row_ref[1], k)
    out_ref[:cut] = first_ref[:, cols] - term[:cut]
    out_ref[cut:] = last_ref[:, cols] - term[cut:]


def lower_three(rest, q_ref, qx_ref, cores_ref, field_ref, row_ref, top_ref, w_ref, k_ref, out_ref):
    child, _ = place(rest)
    side = lax.shift_right_logical(child, 2)
    k = coefficient(3, child, cores_ref, q_ref[...], qx_ref[...])
    k_ref[...] = k
    lefts = jnp.concatenate([row_ref[2], top_ref[side]], 1)
    out_ref[...] = field_ref[...] - dot(lefts, jnp.concatenate([k, w_ref[...]], 0))


def solve_own(rest, own_ref, first_ref, last_ref, row_ref, top_ref, far_ref, *refs):
    *k_refs, out_ref, other_ref = refs
    child, core = place(rest)
    side = lax.shift_right_logical(child, 2)
    out_ref[...] = own_ref[...] - dot(top_ref[1 - side], far_ref[...])
    cols = block(1 - core, far_ref.shape[1])
    cut = first_ref.shape[0]
    lefts = jnp.concatenate([row_ref[1], row_ref[2]], 1)
    term = dot(lefts, jnp.concatenate([ref[...] for ref in k_refs], 0))
    other_ref[:cut] = first_ref[:, cols] - term[:cut]
    other_ref[cut:] = last_ref[:, cols] - term[cut:]


def solve_other(rest, pieces, own_ref, less_ref, top_ref, w_ref, far_ref, out_ref, other_ref, sems):
    child, core = place(rest)
    side = lax.shift_right_logical(child, 2)
    total, half = own_ref.shape
    mine, theirs = block(core, half), block(1 - core, half)
    copies = [pltpu.make_async_copy(own_ref, out_ref.at[:, mine], sems.at[pieces])]
    copies[0].start()
    both = jnp.concatenate([w_ref[...], far_ref[...]], 0)
    step = total // pieces
    for i in range(pieces):
        part = slice(i * step, (i + 1) * step)
        lefts = jnp.concatenate([top_ref[side, part], top_ref[1 - side, part]], 1)
        other_ref[part] = less_ref[part] - dot(lefts, both)
        copy = pltpu.make_async_copy(other_ref.at[part], out_ref.at[part, theirs], sems.at[i])
        copy.start()
        copies.append(copy)
    for copy in copies:
        copy.wait()


def tie(x, *others):
    def body(x_ref, *refs):
        refs[-1][...] = x_ref[...]

    return call(body, shape(*x.shape), (x, *others), 0)


def after(x, *others):
    return lax.optimization_barrier((x, *others))[0]


def swap_wide(x, bit):
    count = lax.axis_size("wide")
    return lax.ppermute(x, "wide", [(w, w ^ (1 << bit)) for w in range(count)])


def swap_narrow(x):
    return lax.ppermute(x, "narrow", [(0, 1), (1, 0)])


def swap_crossed(x, first, second, other_core=False):
    wides, cores = lax.axis_size("wide"), lax.axis_size("narrow")
    route = []
    for w in range(wides):
        for n in range(cores):
            bit = first if n == 0 else second
            route.append((w * cores + n, (w ^ (1 << bit)) * cores + (n ^ other_core)))
    return lax.ppermute(x, ("wide", "narrow"), route)


def swap_diagonal(x, bit):
    return swap_crossed(x, bit, bit, True)


def shards(right_side, leaf_inverse, row_bases, dual_bases, woodbury_cores):
    levels, rows, rank = row_bases.shape
    cols = right_side.shape[1]
    half = cols // 2
    rest = lax.axis_size("wide").bit_length() - 1 - levels
    bit3, bit2, bit1 = rest, rest + 1, rest + 2
    cut = rows // 2

    pieces = 1
    last = call(
        last_product, shape(rank, rank),
        tuple(pltpu.with_memory_space_constraint(x, pltpu.HBM) for x in (dual_bases, row_bases)),
        30 * rows * rows * cols, in_specs=[pl.BlockSpec(memory_space=pltpu.HBM)] * 2,
        scratch=[pltpu.VMEM((rows, rank), F32)] * 2 + [pltpu.SemaphoreType.DMA((pieces, 2))],
    )
    pairs = call(
        pair_products, shape(2 * rank, rank), (dual_bases, row_bases, last), 4 * rows * rank * rank,
    )
    for bit in range(rest):
        pairs, last = pairs + swap_wide(pairs, bit), last + swap_wide(last, bit)
    last_x, pairs_x = swap_diagonal(last, bit3), swap_diagonal(pairs, bit3)

    first_rows = call(
        functools.partial(leaf_rows, 0), shape(cut, cols), (leaf_inverse, after(right_side, last)),
        6 * cut * rows * cols,
    )
    last_z = swap_diagonal(last + after(last_x, first_rows), bit2)
    last_rows, keep, send = call(
        functools.partial(projections, rest),
        (shape(rows - cut, cols),) + (shape(levels * rank, half),) * 2,
        (leaf_inverse, after(right_side, last_x), dual_bases, first_rows), 0,
        scratch=[pltpu.VMEM((levels * rank, rows), BF16)] * 2,
    )
    fix = call(
        functools.partial(pair_corrections, rest), shape(2 * rank, rank),
        (pairs, pairs_x, woodbury_cores), 0,
    )
    recv = swap_narrow(after(send, last_z, fix))
    fix_other = swap_narrow(fix)
    fix_top = call(
        functools.partial(last_corrections, rest), shape(rank, rank),
        (last, last_x, last_z, woodbury_cores), 0,
    )
    fix_top_other = swap_narrow(after(fix_top, fix))
    if rest:
        keep = keep + recv
        for bit in range(rest):
            keep = keep + swap_wide(keep, bit)
        recv = jnp.zeros_like(keep)
    w, v, q = call(
        corrected, (shape(rank, half),) * 3, (keep, recv, fix, fix_other), 18 * rank * rank * half
    )
    w = call(corrected_top, shape(rank, half), (w, v, fix_top, fix_top_other), 0)

    v = tie(v, w)
    v_x = swap_wide(v, bit3)
    top = call(
        functools.partial(top_matrix, rest), shape(2, rows, rank),
        (row_bases, after(woodbury_cores, w)), 0,
    )
    w = w_mid = w + after(swap_crossed(w, bit2, bit3), top, q)
    q = tie(q, top)
    q_x = swap_wide(q, bit3)
    v = v + after(v_x, w_mid)
    v_z = swap_wide(v, bit2)
    w = w + after(swap_crossed(w, bit3, bit2), v)
    far = swap_wide(w, bit1)
    k2, lower = call(
        functools.partial(lower_two, rest), (shape(rank, half), shape(rows, half)),
        (after(v, w), v_z, woodbury_cores, first_rows, last_rows, row_bases), 0,
    )
    k3, lower = call(
        functools.partial(lower_three, rest), (shape(rank, half), shape(rows, half)),
        (q, q_x, woodbury_cores, lower, row_bases, top, w), 0,
    )
    k_other = [swap_narrow(k2), swap_narrow(k3)]
    w_other = swap_narrow(after(w, k2))
    far_other = swap_narrow(far)
    own, less = call(
        functools.partial(solve_own, rest), (shape(rows, half),) * 2,
        (lower, first_rows, last_rows, row_bases, top, far, *k_other), 0,
    )
    pieces = 8
    return call(
        functools.partial(solve_other, rest, pieces), shape(rows, cols),
        (own, less, top, w_other, far_other), 0,
        scratch=[pltpu.VMEM((rows, half), F32), pltpu.SemaphoreType.DMA((pieces + 1,))],
        out_specs=pl.BlockSpec(memory_space=pltpu.HBM),
    )


def solution(mesh):
    return jax.shard_map(
        shards,
        mesh=mesh,
        in_specs=(
            P(("parts", "wide", "narrow"), None),
            P(("parts", "wide", "narrow"), None),
            P(None, ("parts", "wide", "narrow"), None),
            P(None, ("parts", "wide", "narrow"), None),
            P("parts", None),
        ),
        out_specs=P(("parts", "wide", "narrow"), None),
        check_vma=False,
    )
```

```python
import functools

import jax
import jax.numpy as jnp
from jax import lax
from jax.experimental import pallas as pl
from jax.experimental.pallas import tpu as pltpu
from jax.sharding import PartitionSpec as P

F32, BF16 = jnp.float32, jnp.bfloat16
VMEM = pl.BlockSpec(memory_space=pltpu.VMEM)


def halves(x):
    high = x.astype(BF16)
    return high, (x - high.astype(F32)).astype(BF16)


def dot3(a, b, dims=((1,), (0,))):
    def one(x, y):
        return lax.dot_general(x, y, (dims, ((), ())), preferred_element_type=F32)

    return one(a[0], b[0]) + one(a[0], b[1]) + one(a[1], b[0])


def dot(a, b):
    return dot3(halves(a), halves(b))


def dot_t(a, b):
    return dot3(halves(a), halves(b), ((0,), (0,)))


def shape(*dims, dtype=F32):
    return jax.ShapeDtypeStruct(dims, dtype)


def call(body, outs, args, flops, in_specs=None, scratch=(), aliases=None, out_specs=None):
    bytes_accessed = sum(a.size * a.dtype.itemsize for a in args)
    return pl.pallas_call(
        body,
        in_specs=in_specs or [VMEM] * len(args),
        out_specs=jax.tree.map(lambda _: VMEM, outs) if out_specs is None else out_specs,
        out_shape=outs,
        scratch_shapes=list(scratch),
        input_output_aliases=aliases or {},
        compiler_params=pltpu.CompilerParams(vmem_limit_bytes=24 * 2**20),
        cost_estimate=pl.CostEstimate(
            flops=flops, bytes_accessed=0, transcendentals=0
        ),
    )(*args)


def place(rest):
    child = lax.shift_right_logical(lax.axis_index("wide"), rest)
    return child, lax.axis_index("narrow")


def block(index, size):
    return pl.ds(pl.multiple_of(index * size, size), size)


def last_product(dual_hbm, row_hbm, out_ref, dual_ref, row_ref, sems):
    rows = dual_ref.shape[0]
    pieces = sems.shape[0]
    step = rows // pieces
    copies = []
    for i in range(pieces):
        part = pl.ds(i * step, step)
        copies.append((
            pltpu.make_async_copy(dual_hbm.at[0, part], dual_ref.at[part], sems.at[i, 0]),
            pltpu.make_async_copy(row_hbm.at[1, part], row_ref.at[part], sems.at[i, 1]),
        ))
        for copy in copies[-1]:
            copy.start()
    total = jnp.zeros(out_ref.shape, F32)
    for i in range(pieces):
        for copy in copies[i]:
            copy.wait()
        part = slice(i * step, (i + 1) * step)
        total += dot_t(dual_ref[part], row_ref[part])
    out_ref[...] = total


def pair_products(dual_ref, row_ref, last_ref, out_ref):
    rank = row_ref.shape[2]
    both = dot_t(jnp.concatenate([dual_ref[1], dual_ref[0]], 1), row_ref[2])
    out_ref[...] = both


def leaf_rows(start, leaf_ref, right_ref, field_ref):
    rows = field_ref.shape[0]
    step = min(256, rows)
    right = halves(right_ref[...])
    for i in range(0, rows, step):
        field_ref[i:i + step] = dot3(halves(leaf_ref[start + i:start + i + step]), right)


def projections(
    rest, leaf_ref, right_ref, dual_ref, first_ref, last_ref, keep_ref, send_ref, high_ref, low_ref
):
    leaf_rows(first_ref.shape[0], leaf_ref, right_ref, last_ref)
    levels, rows, rank = dual_ref.shape
    for l in range(levels):
        high, low = halves(dual_ref[l].T)
        high_ref[l * rank:(l + 1) * rank] = high
        low_ref[l * rank:(l + 1) * rank] = low
    _, core = place(rest)
    half = keep_ref.shape[1]
    cut = first_ref.shape[0]
    for out, index in ((keep_ref, core), (send_ref, 1 - core)):
        cols = block(index, half)
        top, bottom = halves(first_ref[:, cols]), halves(last_ref[:, cols])
        out[...] = dot3((high_ref[:, :cut], low_ref[:, :cut]), top) + dot3(
            (high_ref[:, cut:], low_ref[:, cut:]), bottom
        )


def pair_corrections(rest, pairs_ref, pairs_x_ref, cores_ref, out_ref):
    rank = pairs_ref.shape[1]
    child, _ = place(rest)
    cols = block(child & 1, rank)
    out_ref[...] = dot(pairs_ref[...], cores_ref[block(6 + child, rank), cols]) + dot(
        pairs_x_ref[...], cores_ref[block(6 + (child ^ 1), rank), cols]
    )


def last_corrections(rest, last_ref, last_x_ref, last_z_ref, cores_ref, out_ref):
    rank = last_ref.shape[0]
    child, _ = place(rest)
    pair = lax.shift_right_logical(child, 1)
    cols = block(pair & 1, rank)
    out_ref[...] = dot(
        last_ref[...] + last_x_ref[...], cores_ref[block(2 + pair, rank), cols]
    ) + dot(last_z_ref[...], cores_ref[block(2 + (pair ^ 1), rank), cols])


def corrected(keep_ref, recv_ref, fix_ref, fix_other_ref, w_ref, v_ref, q_ref):
    rank = v_ref.shape[0]
    q = keep_ref[...] + recv_ref[...]
    q1, q2, q3 = q[:rank], q[rank:2 * rank], q[2 * rank:]
    both = dot(fix_ref[...] + fix_other_ref[...], q3)
    v_ref[...] = q2 - both[:rank]
    w_ref[...] = q1 - both[rank:]
    q_ref[...] = q3


def corrected_top(w_ref, v_ref, fix_ref, fix_other_ref, out_ref):
    out_ref[...] = w_ref[...] - dot(fix_ref[...] + fix_other_ref[...], v_ref[...])


def coefficient(level, child, cores_ref, own, other):
    rank = own.shape[0]
    slot = child & 1
    rows = block(2**level - 2 + child, rank)
    return dot(cores_ref[rows, block(slot, rank)], own) + dot(
        cores_ref[rows, block(1 - slot, rank)], other
    )


def top_matrix(rest, row_ref, cores_ref, out_ref):
    rank = row_ref.shape[2]
    child, _ = place(rest)
    both = dot(row_ref[0], cores_ref[block(lax.shift_right_logical(child, 2), rank)])
    out_ref[0] = both[:, :rank]
    out_ref[1] = both[:, rank:]


def lower_two(rest, v_ref, vz_ref, cores_ref, first_ref, last_ref, row_ref, k_ref, out_ref):
    child, core = place(rest)
    k = coefficient(2, lax.shift_right_logical(child, 1), cores_ref, v_ref[...], vz_ref[...])
    k_ref[...] = k
    cols = block(core, k.shape[1])
    cut = first_ref.shape[0]
    term = dot(row_ref[1], k)
    out_ref[:cut] = first_ref[:, cols] - term[:cut]
    out_ref[cut:] = last_ref[:, cols] - term[cut:]


def lower_three(rest, q_ref, qx_ref, cores_ref, field_ref, row_ref, top_ref, w_ref, k_ref, out_ref):
    child, _ = place(rest)
    side = lax.shift_right_logical(child, 2)
    k = coefficient(3, child, cores_ref, q_ref[...], qx_ref[...])
    k_ref[...] = k
    lefts = jnp.concatenate([row_ref[2], top_ref[side]], 1)
    out_ref[...] = field_ref[...] - dot(lefts, jnp.concatenate([k, w_ref[...]], 0))


def solve_own(rest, own_ref, first_ref, last_ref, row_ref, top_ref, far_ref, *refs):
    *k_refs, out_ref, other_ref = refs
    child, core = place(rest)
    side = lax.shift_right_logical(child, 2)
    out_ref[...] = own_ref[...] - dot(top_ref[1 - side], far_ref[...])
    cols = block(1 - core, far_ref.shape[1])
    cut = first_ref.shape[0]
    lefts = jnp.concatenate([row_ref[1], row_ref[2]], 1)
    term = dot(lefts, jnp.concatenate([ref[...] for ref in k_refs], 0))
    other_ref[:cut] = first_ref[:, cols] - term[:cut]
    other_ref[cut:] = last_ref[:, cols] - term[cut:]


def solve_other(rest, pieces, own_ref, less_ref, top_ref, w_ref, far_ref, out_ref, other_ref, sems):
    child, core = place(rest)
    side = lax.shift_right_logical(child, 2)
    total, half = own_ref.shape
    mine, theirs = block(core, half), block(1 - core, half)
    copies = [pltpu.make_async_copy(own_ref, out_ref.at[:, mine], sems.at[pieces])]
    copies[0].start()
    both = jnp.concatenate([w_ref[...], far_ref[...]], 0)
    step = total // pieces
    for i in range(pieces):
        part = slice(i * step, (i + 1) * step)
        lefts = jnp.concatenate([top_ref[side, part], top_ref[1 - side, part]], 1)
        other_ref[part] = less_ref[part] - dot(lefts, both)
        copy = pltpu.make_async_copy(other_ref.at[part], out_ref.at[part, theirs], sems.at[i])
        copy.start()
        copies.append(copy)
    for copy in copies:
        copy.wait()


def tie(x, *others):
    def body(x_ref, *refs):
        refs[-1][...] = x_ref[...]

    return call(body, shape(*x.shape), (x, *others), 0)


def after(x, *others):
    return lax.optimization_barrier((x, *others))[0]


def swap_wide(x, bit):
    count = lax.axis_size("wide")
    return lax.ppermute(x, "wide", [(w, w ^ (1 << bit)) for w in range(count)])


def swap_narrow(x):
    return lax.ppermute(x, "narrow", [(0, 1), (1, 0)])


def swap_crossed(x, first, second, other_core=False):
    wides, cores = lax.axis_size("wide"), lax.axis_size("narrow")
    route = []
    for w in range(wides):
        for n in range(cores):
            bit = first if n == 0 else second
            route.append((w * cores + n, (w ^ (1 << bit)) * cores + (n ^ other_core)))
    return lax.ppermute(x, ("wide", "narrow"), route)


def swap_diagonal(x, bit):
    return swap_crossed(x, bit, bit, True)


def shards(right_side, leaf_inverse, row_bases, dual_bases, woodbury_cores):
    levels, rows, rank = row_bases.shape
    cols = right_side.shape[1]
    half = cols // 2
    rest = lax.axis_size("wide").bit_length() - 1 - levels
    bit3, bit2, bit1 = rest, rest + 1, rest + 2
    cut = rows // 2

    pieces = 1
    last = call(
        last_product, shape(rank, rank),
        tuple(pltpu.with_memory_space_constraint(x, pltpu.HBM) for x in (dual_bases, row_bases)),
        30 * rows * rows * cols, in_specs=[pl.BlockSpec(memory_space=pltpu.HBM)] * 2,
        scratch=[pltpu.VMEM((rows, rank), F32)] * 2 + [pltpu.SemaphoreType.DMA((pieces, 2))],
    )
    pairs = call(
        pair_products, shape(2 * rank, rank), (dual_bases, row_bases, last), 4 * rows * rank * rank,
    )
    for bit in range(rest):
        pairs, last = pairs + swap_wide(pairs, bit), last + swap_wide(last, bit)
    last_x, pairs_x = swap_diagonal(last, bit3), swap_diagonal(pairs, bit3)

    first_rows = call(
        functools.partial(leaf_rows, 0), shape(cut, cols), (leaf_inverse, after(right_side, last)),
        6 * cut * rows * cols,
    )
    last_z = swap_diagonal(last + after(last_x, first_rows), bit2)
    last_rows, keep, send = call(
        functools.partial(projections, rest),
        (shape(rows - cut, cols),) + (shape(levels * rank, half),) * 2,
        (leaf_inverse, after(right_side, last_x), dual_bases, first_rows), 0,
        scratch=[pltpu.VMEM((levels * rank, rows), BF16)] * 2,
    )
    fix = call(
        functools.partial(pair_corrections, rest), shape(2 * rank, rank),
        (pairs, pairs_x, woodbury_cores), 0,
    )
    recv = swap_narrow(after(send, last_z, fix))
    fix_other = swap_narrow(fix)
    fix_top = call(
        functools.partial(last_corrections, rest), shape(rank, rank),
        (last, last_x, last_z, woodbury_cores), 0,
    )
    fix_top_other = swap_narrow(after(fix_top, fix))
    if rest:
        keep = keep + recv
        for bit in range(rest):
            keep = keep + swap_wide(keep, bit)
        recv = jnp.zeros_like(keep)
    w, v, q = call(
        corrected, (shape(rank, half),) * 3, (keep, recv, fix, fix_other), 18 * rank * rank * half
    )
    w = call(corrected_top, shape(rank, half), (w, v, fix_top, fix_top_other), 0)

    v = tie(v, w)
    v_x = swap_wide(v, bit3)
    top = call(
        functools.partial(top_matrix, rest), shape(2, rows, rank),
        (row_bases, after(woodbury_cores, w)), 0,
    )
    w = w_mid = w + after(swap_crossed(w, bit2, bit3), top)
    v = v + after(v_x, w_mid)
    q_x = swap_wide(after(q, v), bit3)
    v_z = swap_wide(v, bit2)
    w = w + after(swap_crossed(w, bit3, bit2), v)
    far = swap_wide(w, bit1)
    k2, lower = call(
        functools.partial(lower_two, rest), (shape(rank, half), shape(rows, half)),
        (after(v, w), v_z, woodbury_cores, first_rows, last_rows, row_bases), 0,
    )
    k3, lower = call(
        functools.partial(lower_three, rest), (shape(rank, half), shape(rows, half)),
        (q, q_x, woodbury_cores, lower, row_bases, top, w), 0,
    )
    k_other = [swap_narrow(k2), swap_narrow(k3)]
    w_other = swap_narrow(after(w, k2))
    far_other = swap_narrow(far)
    own, less = call(
        functools.partial(solve_own, rest), (shape(rows, half),) * 2,
        (lower, first_rows, last_rows, row_bases, top, far, *k_other), 0,
    )
    pieces = 8
    return call(
        functools.partial(solve_other, rest, pieces), shape(rows, cols),
        (own, less, top, w_other, far_other), 0,
        scratch=[pltpu.VMEM((rows, half), F32), pltpu.SemaphoreType.DMA((pieces + 1,))],
        out_specs=pl.BlockSpec(memory_space=pltpu.HBM),
    )


def solution(mesh):
    return jax.shard_map(
        shards,
        mesh=mesh,
        in_specs=(
            P(("parts", "wide", "narrow"), None),
            P(("parts", "wide", "narrow"), None),
            P(None, ("parts", "wide", "narrow"), None),
            P(None, ("parts", "wide", "narrow"), None),
            P("parts", None),
        ),
        out_specs=P(("parts", "wide", "narrow"), None),
        check_vma=False,
    )
```

```python
import functools

import jax
import jax.numpy as jnp
from jax import lax
from jax.experimental import pallas as pl
from jax.experimental.pallas import tpu as pltpu
from jax.sharding import PartitionSpec as P

F32, BF16 = jnp.float32, jnp.bfloat16
VMEM = pl.BlockSpec(memory_space=pltpu.VMEM)


def halves(x):
    high = x.astype(BF16)
    return high, (x - high.astype(F32)).astype(BF16)


def dot3(a, b, dims=((1,), (0,))):
    def one(x, y):
        return lax.dot_general(x, y, (dims, ((), ())), preferred_element_type=F32)

    return one(a[0], b[0]) + one(a[0], b[1]) + one(a[1], b[0])


def dot(a, b):
    return dot3(halves(a), halves(b))


def dot_t(a, b):
    return dot3(halves(a), halves(b), ((0,), (0,)))


def shape(*dims, dtype=F32):
    return jax.ShapeDtypeStruct(dims, dtype)


def call(body, outs, args, flops, in_specs=None, scratch=(), aliases=None, out_specs=None):
    bytes_accessed = sum(a.size * a.dtype.itemsize for a in args)
    return pl.pallas_call(
        body,
        in_specs=in_specs or [VMEM] * len(args),
        out_specs=jax.tree.map(lambda _: VMEM, outs) if out_specs is None else out_specs,
        out_shape=outs,
        scratch_shapes=list(scratch),
        input_output_aliases=aliases or {},
        compiler_params=pltpu.CompilerParams(vmem_limit_bytes=24 * 2**20),
        cost_estimate=pl.CostEstimate(
            flops=flops, bytes_accessed=0, transcendentals=0
        ),
    )(*args)


def place(rest):
    child = lax.shift_right_logical(lax.axis_index("wide"), rest)
    return child, lax.axis_index("narrow")


def block(index, size):
    return pl.ds(pl.multiple_of(index * size, size), size)


def last_product(dual_hbm, row_hbm, out_ref, dual_ref, row_ref, sems):
    rows = dual_ref.shape[0]
    pieces = sems.shape[0]
    step = rows // pieces
    copies = []
    for i in range(pieces):
        part = pl.ds(i * step, step)
        copies.append((
            pltpu.make_async_copy(dual_hbm.at[0, part], dual_ref.at[part], sems.at[i, 0]),
            pltpu.make_async_copy(row_hbm.at[1, part], row_ref.at[part], sems.at[i, 1]),
        ))
        for copy in copies[-1]:
            copy.start()
    total = jnp.zeros(out_ref.shape, F32)
    for i in range(pieces):
        for copy in copies[i]:
            copy.wait()
        part = slice(i * step, (i + 1) * step)
        total += dot_t(dual_ref[part], row_ref[part])
    out_ref[...] = total


def pair_products(dual_ref, row_ref, last_ref, out_ref):
    rank = row_ref.shape[2]
    both = dot_t(jnp.concatenate([dual_ref[1], dual_ref[0]], 1), row_ref[2])
    out_ref[...] = both


def leaf_rows(start, leaf_ref, right_ref, field_ref):
    rows = field_ref.shape[0]
    step = min(256, rows)
    right = halves(right_ref[...])
    for i in range(0, rows, step):
        field_ref[i:i + step] = dot3(halves(leaf_ref[start + i:start + i + step]), right)


def projections(
    rest, leaf_ref, right_ref, dual_ref, first_ref, last_ref, keep_ref, send_ref, high_ref, low_ref
):
    leaf_rows(first_ref.shape[0], leaf_ref, right_ref, last_ref)
    levels, rows, rank = dual_ref.shape
    for l in range(levels):
        high, low = halves(dual_ref[l].T)
        high_ref[l * rank:(l + 1) * rank] = high
        low_ref[l * rank:(l + 1) * rank] = low
    _, core = place(rest)
    half = keep_ref.shape[1]
    cut = first_ref.shape[0]
    for out, index in ((keep_ref, core), (send_ref, 1 - core)):
        cols = block(index, half)
        top, bottom = halves(first_ref[:, cols]), halves(last_ref[:, cols])
        out[...] = dot3((high_ref[:, :cut], low_ref[:, :cut]), top) + dot3(
            (high_ref[:, cut:], low_ref[:, cut:]), bottom
        )


def pair_corrections(rest, pairs_ref, pairs_x_ref, cores_ref, out_ref):
    rank = pairs_ref.shape[1]
    child, _ = place(rest)
    cols = block(child & 1, rank)
    out_ref[...] = dot(pairs_ref[...], cores_ref[block(6 + child, rank), cols]) + dot(
        pairs_x_ref[...], cores_ref[block(6 + (child ^ 1), rank), cols]
    )


def last_corrections(rest, last_ref, last_x_ref, last_z_ref, cores_ref, out_ref):
    rank = last_ref.shape[0]
    child, _ = place(rest)
    pair = lax.shift_right_logical(child, 1)
    cols = block(pair & 1, rank)
    out_ref[...] = dot(
        last_ref[...] + last_x_ref[...], cores_ref[block(2 + pair, rank), cols]
    ) + dot(last_z_ref[...], cores_ref[block(2 + (pair ^ 1), rank), cols])


def corrected(keep_ref, recv_ref, fix_ref, fix_other_ref, w_ref, v_ref, q_ref):
    rank = v_ref.shape[0]
    q = keep_ref[...] + recv_ref[...]
    q1, q2, q3 = q[:rank], q[rank:2 * rank], q[2 * rank:]
    both = dot(fix_ref[...] + fix_other_ref[...], q3)
    v_ref[...] = q2 - both[:rank]
    w_ref[...] = q1 - both[rank:]
    q_ref[...] = q3


def corrected_top(w_ref, v_ref, fix_ref, fix_other_ref, out_ref):
    out_ref[...] = w_ref[...] - dot(fix_ref[...] + fix_other_ref[...], v_ref[...])


def coefficient(level, child, cores_ref, own, other):
    rank = own.shape[0]
    slot = child & 1
    rows = block(2**level - 2 + child, rank)
    return dot(cores_ref[rows, block(slot, rank)], own) + dot(
        cores_ref[rows, block(1 - slot, rank)], other
    )


def top_matrix(rest, row_ref, cores_ref, out_ref):
    rank = row_ref.shape[2]
    child, _ = place(rest)
    both = dot(row_ref[0], cores_ref[block(lax.shift_right_logical(child, 2), rank)])
    out_ref[0] = both[:, :rank]
    out_ref[1] = both[:, rank:]


def lower_two(rest, v_ref, vz_ref, cores_ref, first_ref, last_ref, row_ref, k_ref, out_ref):
    child, core = place(rest)
    k = coefficient(2, lax.shift_right_logical(child, 1), cores_ref, v_ref[...], vz_ref[...])
    k_ref[...] = k
    cols = block(core, k.shape[1])
    cut = first_ref.shape[0]
    term = dot(row_ref[1], k)
    out_ref[:cut] = first_ref[:, cols] - term[:cut]
    out_ref[cut:] = last_ref[:, cols] - term[cut:]


def lower_three(rest, q_ref, qx_ref, cores_ref, field_ref, row_ref, top_ref, w_ref, k_ref, out_ref):
    child, _ = place(rest)
    side = lax.shift_right_logical(child, 2)
    k = coefficient(3, child, cores_ref, q_ref[...], qx_ref[...])
    k_ref[...] = k
    lefts = jnp.concatenate([row_ref[2], top_ref[side]], 1)
    out_ref[...] = field_ref[...] - dot(lefts, jnp.concatenate([k, w_ref[...]], 0))


def solve_own(rest, own_ref, first_ref, last_ref, row_ref, top_ref, far_ref, *refs):
    *k_refs, out_ref, other_ref = refs
    child, core = place(rest)
    side = lax.shift_right_logical(child, 2)
    out_ref[...] = own_ref[...] - dot(top_ref[1 - side], far_ref[...])
    cols = block(1 - core, far_ref.shape[1])
    cut = first_ref.shape[0]
    lefts = jnp.concatenate([row_ref[1], row_ref[2]], 1)
    term = dot(lefts, jnp.concatenate([ref[...] for ref in k_refs], 0))
    other_ref[:cut] = first_ref[:, cols] - term[:cut]
    other_ref[cut:] = last_ref[:, cols] - term[cut:]


def solve_other(rest, pieces, own_ref, less_ref, top_ref, w_ref, far_ref, out_ref, other_ref, sems):
    child, core = place(rest)
    side = lax.shift_right_logical(child, 2)
    total, half = own_ref.shape
    mine, theirs = block(core, half), block(1 - core, half)
    copies = [pltpu.make_async_copy(own_ref, out_ref.at[:, mine], sems.at[pieces])]
    copies[0].start()
    both = jnp.concatenate([w_ref[...], far_ref[...]], 0)
    step = total // pieces
    for i in range(pieces):
        part = slice(i * step, (i + 1) * step)
        lefts = jnp.concatenate([top_ref[side, part], top_ref[1 - side, part]], 1)
        other_ref[part] = less_ref[part] - dot(lefts, both)
        copy = pltpu.make_async_copy(other_ref.at[part], out_ref.at[part, theirs], sems.at[i])
        copy.start()
        copies.append(copy)
    for copy in copies:
        copy.wait()


def tie(x, *others):
    def body(x_ref, *refs):
        refs[-1][...] = x_ref[...]

    return call(body, shape(*x.shape), (x, *others), 0)


def after(x, *others):
    return lax.optimization_barrier((x, *others))[0]


def swap_wide(x, bit):
    count = lax.axis_size("wide")
    return lax.ppermute(x, "wide", [(w, w ^ (1 << bit)) for w in range(count)])


def swap_narrow(x):
    return lax.ppermute(x, "narrow", [(0, 1), (1, 0)])


def swap_crossed(x, first, second, other_core=False):
    wides, cores = lax.axis_size("wide"), lax.axis_size("narrow")
    route = []
    for w in range(wides):
        for n in range(cores):
            bit = first if n == 0 else second
            route.append((w * cores + n, (w ^ (1 << bit)) * cores + (n ^ other_core)))
    return lax.ppermute(x, ("wide", "narrow"), route)


def swap_diagonal(x, bit):
    return swap_crossed(x, bit, bit, True)


def shards(right_side, leaf_inverse, row_bases, dual_bases, woodbury_cores):
    levels, rows, rank = row_bases.shape
    cols = right_side.shape[1]
    half = cols // 2
    rest = lax.axis_size("wide").bit_length() - 1 - levels
    bit3, bit2, bit1 = rest, rest + 1, rest + 2
    cut = rows // 2

    pieces = 1
    last = call(
        last_product, shape(rank, rank),
        tuple(pltpu.with_memory_space_constraint(x, pltpu.HBM) for x in (dual_bases, row_bases)),
        30 * rows * rows * cols, in_specs=[pl.BlockSpec(memory_space=pltpu.HBM)] * 2,
        scratch=[pltpu.VMEM((rows, rank), F32)] * 2 + [pltpu.SemaphoreType.DMA((pieces, 2))],
    )
    pairs = call(
        pair_products, shape(2 * rank, rank), (dual_bases, row_bases, last), 4 * rows * rank * rank,
    )
    for bit in range(rest):
        pairs, last = pairs + swap_wide(pairs, bit), last + swap_wide(last, bit)
    last_x, pairs_x = swap_diagonal(last, bit3), swap_diagonal(pairs, bit3)

    first_rows = call(
        functools.partial(leaf_rows, 0), shape(cut, cols), (leaf_inverse, after(right_side, last)),
        6 * cut * rows * cols,
    )
    last_z = swap_diagonal(last + after(last_x, first_rows), bit2)
    last_rows, keep, send = call(
        functools.partial(projections, rest),
        (shape(rows - cut, cols),) + (shape(levels * rank, half),) * 2,
        (leaf_inverse, after(right_side, last_x), dual_bases, first_rows), 0,
        scratch=[pltpu.VMEM((levels * rank, rows), BF16)] * 2,
    )
    fix = call(
        functools.partial(pair_corrections, rest), shape(2 * rank, rank),
        (pairs, pairs_x, woodbury_cores), 0,
    )
    recv = swap_narrow(after(send, last_z, fix))
    fix_other = swap_narrow(fix)
    fix_top = call(
        functools.partial(last_corrections, rest), shape(rank, rank),
        (last, last_x, last_z, woodbury_cores), 0,
    )
    fix_top_other = swap_narrow(after(fix_top, fix))
    if rest:
        keep = keep + recv
        for bit in range(rest):
            keep = keep + swap_wide(keep, bit)
        recv = jnp.zeros_like(keep)
    w, v, q = call(
        corrected, (shape(rank, half),) * 3, (keep, recv, fix, fix_other), 18 * rank * rank * half
    )
    w = call(corrected_top, shape(rank, half), (w, v, fix_top, fix_top_other), 0)

    v = tie(v, w)
    v_x = swap_wide(v, bit3)
    top = call(
        functools.partial(top_matrix, rest), shape(2, rows, rank),
        (row_bases, after(woodbury_cores, w)), 0,
    )
    w = w_mid = w + after(swap_crossed(w, bit2, bit3), top)
    v = v + after(v_x, w_mid)
    q_x = swap_wide(after(q, v), bit3)
    v_z = swap_wide(v, bit2)
    w = w + after(swap_crossed(w, bit3, bit2), v)
    far = swap_wide(w, bit1)
    k2, lower = call(
        functools.partial(lower_two, rest), (shape(rank, half), shape(rows, half)),
        (after(v, w), v_z, woodbury_cores, first_rows, last_rows, row_bases), 0,
    )
    k3, lower = call(
        functools.partial(lower_three, rest), (shape(rank, half), shape(rows, half)),
        (q, q_x, woodbury_cores, lower, row_bases, top, w), 0,
    )
    k_other = [swap_narrow(k2), swap_narrow(k3)]
    w_other = swap_narrow(after(w, k3))
    far_other = swap_narrow(far)
    own, less = call(
        functools.partial(solve_own, rest), (shape(rows, half),) * 2,
        (lower, first_rows, last_rows, row_bases, top, far, *k_other), 0,
    )
    pieces = 8
    return call(
        functools.partial(solve_other, rest, pieces), shape(rows, cols),
        (own, less, top, w_other, far_other), 0,
        scratch=[pltpu.VMEM((rows, half), F32), pltpu.SemaphoreType.DMA((pieces + 1,))],
        out_specs=pl.BlockSpec(memory_space=pltpu.HBM),
    )


def solution(mesh):
    return jax.shard_map(
        shards,
        mesh=mesh,
        in_specs=(
            P(("parts", "wide", "narrow"), None),
            P(("parts", "wide", "narrow"), None),
            P(None, ("parts", "wide", "narrow"), None),
            P(None, ("parts", "wide", "narrow"), None),
            P("parts", None),
        ),
        out_specs=P(("parts", "wide", "narrow"), None),
        check_vma=False,
    )
```
